32 devices in a mesh: dp: 8 (over z, y), tensor: 4 (over x, core).
Axes of the slice: x: 2, y: 2, z: 4, core: 2. Of those that a mesh axis runs over, the one named last changes fastest.
Arguments:
- tokens: bfloat16 [8192, 1024], P('dp')
- cotangent: bfloat16 [8192, 1024], P('dp'), may hold values from -6 to 6
- segments: int32 [8192], P('dp'), may hold values from 0 to 5, as said below
- positions: int32 [8192], P('dp'), may hold values from 0 to 5094, as said below
- attn_gain: bfloat16 [1024], P('dp'), may hold values from 0.099609375 to 1.8984375
- w_query: bfloat16 [1024, 1024], P('dp', 'tensor'), may hold values from -0.1875 to 0.1875
- w_key: bfloat16 [1024, 512], P('dp', 'tensor'), may hold values from -0.1875 to 0.1875
- w_value: bfloat16 [1024, 512], P('dp', 'tensor'), may hold values from -0.1875 to 0.1875
- query_gain: bfloat16 [64], P('dp'), may hold values from 0.5 to 2
- key_gain: bfloat16 [64], P('dp'), may hold values from 0.5 to 2
- w_out: bfloat16 [1024, 1024], P('tensor', 'dp'), may hold values from -1.5 to 1.5
- ffn_gain: bfloat16 [1024], P('dp'), may hold values from 0.099609375 to 1.8984375
- w_gate: bfloat16 [1024, 4608], P('dp', 'tensor'), may hold values from -0.1875 to 0.1875
- w_up: bfloat16 [1024, 4608], P('dp', 'tensor'), may hold values from -0.1875 to 0.1875
- w_down: bfloat16 [4608, 1024], P('tensor', 'dp'), may hold values from -0.1875 to 0.1875
Outputs:
- output: bfloat16 [8192, 1024], P(('dp', 'tensor'))
- tokens_grad: float32 [8192, 1024], P('dp')
- attn_gain_grad: float32 [1024], P('dp')
- query_grad: float32 [1024, 1024], P('dp', 'tensor')
- key_grad: float32 [1024, 512], P('dp', 'tensor')
- value_grad: float32 [1024, 512], P('dp', 'tensor')
- query_gain_grad: float32 [64], P('dp')
- key_gain_grad: float32 [64], P('dp')
- out_grad: float32 [1024, 1024], P('tensor', 'dp')
- ffn_gain_grad: float32 [1024], P('dp')
- gate_grad: float32 [1024, 4608], P('dp', 'tensor')
- up_grad: float32 [1024, 4608], P('dp', 'tensor')
- down_grad: float32 [4608, 1024], P('tensor', 'dp')
The draws below stay inside these ranges and needn't reach their ends.
Inputs may be any that keep to these rules, and one draw needn't show every extreme that they name: `segments`: within each sequence of 1024 tokens the numbers start at 0 and never fall; every run but a sequence's last is a document of 200 to 1000 tokens, the last is at most 1000. Within a document the positions rise by one from token to token; a document's first position lies below 4096.
All inputs are finite; a program needn't handle non-finite values.
Results may differ from the reference program's by a relative error of at most 0.028.
Values may be sent and summed in bfloat16 or wider, within the bound.
A program may use at most 192 MiB of HBM per device.

```python
import math
import jax
import jax.numpy as jnp
from jax import lax

D = 1024
HEADS = 16
KV = 8
HD = 64
FF = 4608
LEN = 1024
DOC_MIN = 200
DOC_MAX = 1000
SEQS = 8
TOKENS = 8192


def doc_layout(key):
    per_seq = LEN // DOC_MIN + 1
    lengths = jax.random.randint(jax.random.fold_in(key, 11), (SEQS, per_seq), DOC_MIN, DOC_MAX + 1)
    offsets = jax.random.randint(jax.random.fold_in(key, 12), (SEQS, per_seq), 0, 4 * LEN)
    chosen = jax.random.randint(jax.random.fold_in(key, 13), (), 0, SEQS)
    following = (chosen + 1) % SEQS
    seq_ids = jnp.arange(SEQS, dtype=jnp.int32)[:, None]
    doc_ids = jnp.arange(per_seq, dtype=jnp.int32)[None, :]
    lengths = jnp.where(seq_ids == chosen, DOC_MIN, lengths)
    first_long = (seq_ids == following) & (doc_ids == 0)
    lengths = jnp.where(first_long, DOC_MAX, lengths)
    offsets = jnp.where(first_long, 4 * LEN - 1, offsets)
    offsets = jnp.where((seq_ids == chosen) & (doc_ids == 0), 0, offsets)
    ends = jnp.cumsum(lengths, axis=1)
    starts = ends - lengths
    places = jnp.arange(LEN, dtype=jnp.int32)
    seg_ids = jnp.sum((ends[:, None, :] <= places[None, :, None]).astype(jnp.int32), axis=2)
    onehot = (seg_ids[:, :, None] == jnp.arange(per_seq, dtype=jnp.int32)[None, None, :]).astype(jnp.int32)
    start_tok = jnp.sum(onehot * starts[:, None, :], axis=2)
    offset_tok = jnp.sum(onehot * offsets[:, None, :], axis=2)
    place_ids = places[None, :] - start_tok + offset_tok
    return (seg_ids.reshape(-1).astype(jnp.int32), place_ids.reshape(-1).astype(jnp.int32))


def draw_segments(key, part):
    seg_ids, place_ids = doc_layout(key)
    return seg_ids


def draw_positions(key, part):
    seg_ids, place_ids = doc_layout(key)
    return place_ids


def draw_tokens(key, part):
    key = jax.random.fold_in(key, 3)
    row_key, col_key, base_key = jax.random.split(key, 3)
    row_scale = jnp.exp(jax.random.uniform(row_key, (TOKENS, 1), dtype=jnp.float32, minval=math.log(0.3), maxval=math.log(3.0)))
    col_scale = jnp.exp(jax.random.uniform(col_key, (1, D), dtype=jnp.float32, minval=math.log(0.3), maxval=math.log(3.0)))
    values = jax.random.normal(base_key, (TOKENS, D), dtype=jnp.float32) * row_scale * col_scale
    return values.astype(jnp.bfloat16)


def level_of(own_key, shape, shards, low, high):
    loudness, own = 1.0, jax.random.fold_in(own_key, 6)
    for dim, parts in shards:
        heights = jnp.exp(jax.random.uniform(jax.random.fold_in(own, dim), (parts,), jnp.float32, low / len(shards), high / len(shards)))
        loudness = loudness * jnp.repeat(heights, shape[dim] // parts).reshape([-1 if axis == dim else 1 for axis in range(len(shape))])
    return loudness


def gaussian(stream_key, shape, scale, limit, cuts=(), kind=jnp.bfloat16):
    entries = jax.random.normal(stream_key, shape, jnp.float32) * scale
    if len(cuts) > 0:
        entries = level_of(stream_key, shape, cuts, -0.22, 0.18) * entries
    return jnp.clip(entries, min=-limit, max=limit).astype(kind)


def setup_inputs(seed: int = 0) -> dict:
    streams_of = jax.random.split(jax.random.key(seed), 16)
    tokens = draw_tokens(jax.random.fold_in(streams_of[15], 71), 0)
    cotangent = gaussian(streams_of[1], (TOKENS, D), 1.0, 6.0, ((0, 8),))
    segments = draw_segments(jax.random.fold_in(streams_of[15], 71), 0)
    positions = draw_positions(jax.random.fold_in(streams_of[15], 71), 0)
    attn_gain = jnp.clip(1.0 + 0.18 * jax.random.normal(streams_of[4], (D,), jnp.float32), 0.099609375, 1.8984375).astype(jnp.bfloat16)
    w_query = gaussian(streams_of[5], (D, HEADS * HD), D ** -0.5, 0.1875, ((0, 8), (1, 4)))
    w_key = gaussian(streams_of[6], (D, KV * HD), D ** -0.5, 0.1875, ((0, 8), (1, 4)))
    w_value = gaussian(streams_of[7], (D, KV * HD), D ** -0.5, 0.1875, ((0, 8), (1, 4)))
    query_gain = jnp.clip(0.5 + 1.5 * jax.random.uniform(streams_of[8], (HD,), jnp.float32) ** level_of(streams_of[8], (HD,), ((0, 8),), -0.2, 0.2), 0.5, 2.0).astype(jnp.bfloat16)
    key_gain = jnp.clip(0.5 + 1.5 * jax.random.uniform(streams_of[9], (HD,), jnp.float32) ** level_of(streams_of[9], (HD,), ((0, 8),), -0.2, 0.2), 0.5, 2.0).astype(jnp.bfloat16)
    w_out = gaussian(streams_of[10], (HEADS * HD, D), (HEADS * HD // 64) ** -0.5, 1.5, ((0, 4), (1, 8)))
    ffn_gain = jnp.clip(1.0 + 0.18 * jax.random.normal(streams_of[11], (D,), jnp.float32), 0.099609375, 1.8984375).astype(jnp.bfloat16)
    w_gate = gaussian(streams_of[12], (D, FF), D ** -0.5, 0.1875, ((0, 8), (1, 4)))
    w_up = gaussian(streams_of[13], (D, FF), D ** -0.5, 0.1875, ((0, 8), (1, 4)))
    w_down = gaussian(streams_of[14], (FF, D), (FF // 4) ** -0.5, 0.1875, ((0, 4), (1, 8)))
    return dict(tokens=tokens, cotangent=cotangent, segments=segments, positions=positions, attn_gain=attn_gain, w_query=w_query, w_key=w_key, w_value=w_value, query_gain=query_gain, key_gain=key_gain, w_out=w_out, ffn_gain=ffn_gain, w_gate=w_gate, w_up=w_up, w_down=w_down)


EPSILON = 1e-05
ROPE_BASE = 1000000.0
MASKED = -1e+30

@jax.custom_vjp
def low(v):
    return lax.optimization_barrier(v.astype(jnp.bfloat16)).astype(jnp.float32)

@jax.custom_vjp
def low_back(v):
    return v

def low_keep(v):
    return (low(v), None)

def low_pass(kept, grad):
    return (grad,)

def back_keep(v):
    return (v, None)

def back_low(kept, grad):
    return (low(grad),)
low.defvjp(low_keep, low_pass)
low_back.defvjp(back_keep, back_low)

def rms_scale(values, gain):
    return values * lax.rsqrt(lax.optimization_barrier(jnp.mean(values * values, axis=-1, keepdims=True)) + EPSILON) * gain

def rotate_half(values, cosine, sine_table):
    halfway = values.shape[-1] // 2
    first_half = values[..., :halfway]
    second_half = values[..., halfway:]
    return jnp.concatenate([first_half * cosine - second_half * sine_table, second_half * cosine + first_half * sine_table], axis=-1)

def rope_tables(positions):
    halfway = HD // 2
    frequency = ROPE_BASE ** (-(jnp.arange(halfway, dtype=jnp.float32) * 2.0 / HD))
    angle_grid = positions.astype(jnp.float32)[:, None] * frequency[None, :]
    return (jnp.cos(angle_grid)[:, None, :], jnp.sin(angle_grid)[:, None, :])

def product(left, right):
    return jnp.dot(left, right, precision=lax.Precision.HIGHEST)

def forward(token_rows, seq_segments, seq_positions, params):
    attn_gain, w_query, w_key, w_value, query_gain, key_gain, w_out, ffn_gain, w_gate, w_up, w_down = params
    length = token_rows.shape[0]
    group_size = HEADS // KV
    normed = low(rms_scale(token_rows, attn_gain))
    query_raw = low_back(product(normed, w_query)).reshape(length, HEADS, HD)
    key_raw = low_back(product(normed, w_key)).reshape(length, KV, HD)
    value_rows = low(low_back(product(normed, w_value))).reshape(length, KV, HD)
    cosine, sine_table = rope_tables(seq_positions)
    queries = low(rotate_half(rms_scale(query_raw, query_gain), cosine, sine_table)).reshape(length, KV, group_size, HD)
    keys_low = low(rotate_half(rms_scale(key_raw, key_gain), cosine, sine_table))
    scores = low_back(jnp.einsum('tkgd,skd->kgts', queries, keys_low, precision=lax.Precision.HIGHEST) * HD ** (-0.5))
    places = jnp.arange(length)
    allowed = (places[:, None] >= places[None, :]) & (seq_segments[:, None] == seq_segments[None, :])
    scores = jnp.where(allowed, scores, MASKED)
    soft_weights = low(jax.nn.softmax(scores, axis=-1))
    mixed = jnp.einsum('kgts,skd->tkgd', soft_weights, value_rows, precision=lax.Precision.HIGHEST).reshape(length, HEADS * HD)
    mixed = low(low_back(mixed))
    residual = token_rows + low_back(product(mixed, w_out))
    normed_ffn = low(rms_scale(residual, ffn_gain))
    gate_value = low_back(product(normed_ffn, w_gate))
    up_value = low_back(product(normed_ffn, w_up))
    hidden = low(jax.nn.silu(gate_value) * up_value)
    return residual + low_back(product(hidden, w_down))

def reference(tokens, cotangent, segments, positions, attn_gain, w_query, w_key, w_value, query_gain, key_gain, w_out, ffn_gain, w_gate, w_up, w_down):
    weights = tuple((member.astype(jnp.float32) for member in (attn_gain, w_query, w_key, w_value, query_gain, key_gain, w_out, ffn_gain, w_gate, w_up, w_down)))
    seq_count = tokens.shape[0] // LEN
    inputs = (tokens.astype(jnp.float32).reshape(seq_count, LEN, D), cotangent.astype(jnp.float32).reshape(seq_count, LEN, D), segments.reshape(seq_count, LEN), positions.reshape(seq_count, LEN))

    def one_sequence(totals, member):
        token_rows, grad_rows, seq_segments, seq_positions = member

        def apply_block(rows_in, params):
            return forward(rows_in, seq_segments, seq_positions, params)
        result, pull_back = jax.vjp(apply_block, token_rows, weights)
        grad_tokens, grad_params = pull_back(grad_rows)
        totals = tuple((older + newer for older, newer in zip(totals, grad_params)))
        return (totals, (result.astype(jnp.bfloat16), grad_tokens))
    start_totals = tuple((jnp.zeros_like(member) for member in weights))
    totals, (outputs, token_grads) = lax.scan(one_sequence, start_totals, inputs)
    return (outputs.reshape(-1, D), token_grads.reshape(-1, D), totals[0], totals[1], totals[2], totals[3], totals[4], totals[5], totals[6], totals[7], totals[8], totals[9], totals[10])
```

```python
import functools

import jax
import jax.numpy as jnp
from jax import lax
from jax.experimental import pallas as pl
from jax.experimental.pallas import tpu as pltpu
from jax.sharding import PartitionSpec as P

HD = 64
LEN = 1024


EPSILON = 1e-05
ROPE_BASE = 1000000.0
MASKED = -1e30


def norm_rows(values, gain):
    return values * lax.rsqrt(jnp.mean(values * values, axis=-1, keepdims=True) + EPSILON) * gain


def rotate_half(values, cosine, sine_table):
    halfway = values.shape[-1] // 2
    first_half = values[..., :halfway]
    second_half = values[..., halfway:]
    return jnp.concatenate(
        [
            first_half * cosine - second_half * sine_table,
            second_half * cosine + first_half * sine_table,
        ],
        axis=-1,
    )


def rope_tables(positions):
    halfway = HD // 2
    frequency = ROPE_BASE ** (-(jnp.arange(halfway, dtype=jnp.float32) * 2.0 / HD))
    angle_grid = positions.astype(jnp.float32)[:, None] * frequency[None, :]
    return (jnp.cos(angle_grid)[:, None, :], jnp.sin(angle_grid)[:, None, :])


def matmul(left, right):
    return jnp.dot(left, right, preferred_element_type=jnp.float32)


def matmul_tn(left, right):
    return lax.dot_general(
        left, right, (((0,), (0,)), ((), ())), preferred_element_type=jnp.float32
    )


def matmul_nt(left, right):
    return lax.dot_general(
        left, right, (((1,), (1,)), ((), ())), preferred_element_type=jnp.float32
    )


def block_scores(query_block, key_rows, seq_segments, first_row, last_row):
    score_scale = query_block.shape[-1] ** (-0.5)
    places = jnp.arange(seq_segments.shape[0])
    scores = (
        jnp.einsum("tkgd,skd->kgts", query_block, key_rows, preferred_element_type=jnp.float32)
        * score_scale
    )
    allowed = (places[first_row:last_row, None] >= places[None, :last_row]) & (
        seq_segments[first_row:last_row, None] == seq_segments[None, :last_row]
    )
    return jnp.where(allowed, scores, MASKED)


def attend(operands):
    queries, keys_low, values_low, seq_segments = operands
    length = queries.shape[0]
    block_rows = min(512, length)
    pieces = []
    lse_parts = []
    for first_row in range(0, length, block_rows):
        last_row = first_row + block_rows
        scores = block_scores(
            queries[first_row:last_row], keys_low[:last_row], seq_segments, first_row, last_row
        )
        row_max = jnp.max(scores, axis=-1, keepdims=True)
        shifted = jnp.exp(scores - row_max)
        totals = jnp.sum(shifted, axis=-1, keepdims=True)
        probabilities = (shifted / totals).astype(jnp.bfloat16)
        pieces.append(
            jnp.einsum(
                "kgts,skd->tkgd",
                probabilities,
                values_low[:last_row],
                preferred_element_type=jnp.float32,
            )
        )
        lse_parts.append(row_max + jnp.log(totals))
    return (jnp.concatenate(pieces, axis=0), jnp.concatenate(lse_parts, axis=2))


def attend_back(operands):
    queries, keys_low, values_low, seq_segments, lse_rows, grad_mixed = operands
    length = queries.shape[0]
    block_rows = min(512, length)
    score_scale = queries.shape[-1] ** (-0.5)
    key_total = jnp.zeros(keys_low.shape, jnp.float32)
    value_total = jnp.zeros(values_low.shape, jnp.float32)
    query_pieces = []
    for first_row in range(0, length, block_rows):
        last_row = first_row + block_rows
        scores = block_scores(
            queries[first_row:last_row], keys_low[:last_row], seq_segments, first_row, last_row
        )
        probabilities = jnp.exp(scores - lse_rows[:, :, first_row:last_row])
        grad_block = grad_mixed[first_row:last_row]
        grad_probs = jnp.einsum(
            "tkgd,skd->kgts", grad_block, values_low[:last_row], preferred_element_type=jnp.float32
        )
        row_terms = jnp.sum(probabilities * grad_probs, axis=-1, keepdims=True)
        grad_scores = (probabilities * (grad_probs - row_terms)).astype(jnp.bfloat16)
        query_pieces.append(
            jnp.einsum(
                "kgts,skd->tkgd",
                grad_scores,
                keys_low[:last_row],
                preferred_element_type=jnp.float32,
            )
            * score_scale
        )
        padding = ((0, length - last_row), (0, 0), (0, 0))
        key_part = (
            jnp.einsum(
                "kgts,tkgd->skd",
                grad_scores,
                queries[first_row:last_row],
                preferred_element_type=jnp.float32,
            )
            * score_scale
        )
        value_part = jnp.einsum(
            "kgts,tkgd->skd",
            probabilities.astype(jnp.bfloat16),
            grad_block,
            preferred_element_type=jnp.float32,
        )
        key_total = key_total + jnp.pad(key_part, padding)
        value_total = value_total + jnp.pad(value_part, padding)
    return (jnp.concatenate(query_pieces, axis=0), key_total, value_total)


MESH = pl.DeviceIdType.MESH
VMEM_BYTES = 44 * 1024 * 1024


def block_of(ref, place, size):
    return ref.at[pl.ds(pl.multiple_of(place * size, size), size), :]


def greet(peers):
    barrier = pltpu.get_barrier_semaphore()
    for peer in peers:
        pl.semaphore_signal(barrier, inc=1, device_id=peer, device_id_type=MESH)
    pl.semaphore_wait(barrier, len(peers))


def dp_places(size):
    me = lax.axis_index("dp")
    return me // 2, lax.rem(me, 2), size // 2


def gather_kernel(size, count, *refs):
    shards, wholes = refs[:count], refs[count : 2 * count]
    own_sem, far_send, far_recv, near_send, near_recv = refs[2 * count :]
    column, side, columns = dp_places(size)
    near = {"dp": column * 2 + 1 - side}
    far = [{"dp": lax.rem(column + k, columns) * 2 + side} for k in range(1, columns)]
    greet([near] + far)
    mine = column * 2 + side
    started = []

    def slot(a, place):
        return block_of(wholes[a], place, shards[a].shape[0])

    for a in range(count):
        own = pltpu.make_async_copy(shards[a], slot(a, mine), own_sem.at[a])
        own.start()
        started.append(own.wait)
        copy = pltpu.make_async_remote_copy(
            src_ref=shards[a], dst_ref=slot(a, mine),
            send_sem=near_send.at[a, 0], recv_sem=near_recv.at[a, 0],
            device_id=near, device_id_type=MESH,
        )
        copy.start()
        started.append(copy.wait)
    arrivals = []
    for k in range(1, columns):
        for a in range(count):
            copy = pltpu.make_async_remote_copy(
                src_ref=shards[a], dst_ref=slot(a, mine),
                send_sem=far_send.at[a, k - 1], recv_sem=far_recv.at[a, k - 1],
                device_id=far[k - 1], device_id_type=MESH,
            )
            copy.start()
            started.append(copy.wait_send)
            arrivals.append((k, a))
    for k, a in arrivals:
        place = lax.rem(column + columns - k, columns) * 2 + side
        landed = pltpu.make_async_remote_copy(
            src_ref=shards[a], dst_ref=slot(a, place),
            send_sem=far_send.at[a, k - 1], recv_sem=far_recv.at[a, k - 1],
            device_id=near, device_id_type=MESH,
        )
        landed.wait_recv()
        copy = pltpu.make_async_remote_copy(
            src_ref=slot(a, place), dst_ref=slot(a, place),
            send_sem=near_send.at[a, k], recv_sem=near_recv.at[a, k],
            device_id=near, device_id_type=MESH,
        )
        copy.start()
        started.append(copy.wait)
    for wait in started:
        wait()


def gather_dp(arrays, collective_id):
    size = lax.axis_size("dp")
    columns, count = size // 2, len(arrays)
    shapes = [
        jax.ShapeDtypeStruct((size * array.shape[0], array.shape[1]), array.dtype)
        for array in arrays
    ]
    dma = pltpu.SemaphoreType.DMA
    return pl.pallas_call(
        functools.partial(gather_kernel, size, count),
        out_shape=tuple(shapes),
        in_specs=[pl.BlockSpec(memory_space=pl.ANY)] * count,
        out_specs=tuple([pl.BlockSpec(memory_space=pl.ANY)] * count),
        scratch_shapes=[
            dma((count,)),
            dma((count, columns - 1)),
            dma((count, columns - 1)),
            dma((count, columns)),
            dma((count, columns)),
        ],
        compiler_params=pltpu.CompilerParams(collective_id=collective_id, has_side_effects=True),
    )(*arrays)


def scatter_kernel(size, count, *refs):
    parts, sums = refs[:count], refs[count : 2 * count]
    near_slots = refs[2 * count : 3 * count]
    leaving = refs[3 * count : 4 * count]
    far_slots = refs[4 * count : 5 * count]
    near_send, near_recv, far_send, far_recv = refs[5 * count :]
    column, side, columns = dp_places(size)
    near = {"dp": column * 2 + 1 - side}
    far = [{"dp": lax.rem(column + k, columns) * 2 + side} for k in range(1, columns)]
    greet([near] + far)
    order = [(k, a) for k in list(range(1, columns)) + [0] for a in range(count)]

    def part(a, place):
        return block_of(parts[a], place, sums[a].shape[0])

    near_copies, far_copies = {}, {}
    for k, a in order:
        place = lax.rem(column + k, columns) * 2 + 1 - side
        copy = pltpu.make_async_remote_copy(
            src_ref=part(a, place), dst_ref=near_slots[a].at[k],
            send_sem=near_send.at[a, k], recv_sem=near_recv.at[a, k],
            device_id=near, device_id_type=MESH,
        )
        copy.start()
        near_copies[k, a] = copy
    for k, a in order:
        near_copies[k, a].wait_recv()
        place = lax.rem(column + k, columns) * 2 + side
        total = part(a, place)[...].astype(jnp.float32) + near_slots[a][k].astype(jnp.float32)
        if k == 0:
            sums[a][...] = total
            continue
        leaving[a][k - 1] = total.astype(jnp.bfloat16)
        copy = pltpu.make_async_remote_copy(
            src_ref=leaving[a].at[k - 1], dst_ref=far_slots[a].at[k - 1],
            send_sem=far_send.at[a, k - 1], recv_sem=far_recv.at[a, k - 1],
            device_id=far[k - 1], device_id_type=MESH,
        )
        copy.start()
        far_copies[k, a] = copy
    for k, a in order:
        if k > 0:
            far_copies[k, a].wait_recv()
            sums[a][...] += far_slots[a][k - 1].astype(jnp.float32)
    for k, a in order:
        near_copies[k, a].wait_send()
        if k > 0:
            far_copies[k, a].wait_send()


def scatter_dp(arrays, collective_id):
    size = lax.axis_size("dp")
    columns, count = size // 2, len(arrays)
    shapes = [(array.shape[0] // size, array.shape[1]) for array in arrays]
    dma = pltpu.SemaphoreType.DMA
    return pl.pallas_call(
        functools.partial(scatter_kernel, size, count),
        out_shape=tuple(jax.ShapeDtypeStruct(shape, jnp.float32) for shape in shapes),
        in_specs=[pl.BlockSpec(memory_space=pltpu.VMEM)] * count,
        out_specs=tuple([pl.BlockSpec(memory_space=pltpu.VMEM)] * count),
        scratch_shapes=[pltpu.VMEM((columns,) + shape, jnp.bfloat16) for shape in shapes]
        + [pltpu.VMEM((columns - 1,) + shape, jnp.bfloat16) for shape in shapes]
        + [pltpu.VMEM((columns - 1,) + shape, jnp.bfloat16) for shape in shapes]
        + [
            dma((count, columns)),
            dma((count, columns)),
            dma((count, columns - 1)),
            dma((count, columns - 1)),
        ],
        compiler_params=pltpu.CompilerParams(
            collective_id=collective_id, has_side_effects=True, vmem_limit_bytes=VMEM_BYTES
        ),
    )(*arrays)


def total_kernel(size, *refs):
    (part, small, whole, small_sum, near_slots, leaving, far_slots, small_slots,
     near_send, near_recv, far_send, far_recv, back_send, back_recv, on_send, on_recv,
     small_send, small_recv) = refs
    me = lax.axis_index("tensor")
    column, side, columns = me // 2, lax.rem(me, 2), size // 2
    share = whole.shape[0] // size
    near = {"tensor": column * 2 + 1 - side}
    far = [{"tensor": lax.rem(column + k, columns) * 2 + side} for k in range(1, columns)]
    others = [{"tensor": lax.rem(me + k, size)} for k in range(1, size)]
    greet(others)

    def rows(ref, place):
        return block_of(ref, place, share)

    small_copies = []
    for k in range(1, size):
        copy = pltpu.make_async_remote_copy(
            src_ref=small, dst_ref=small_slots.at[k - 1],
            send_sem=small_send.at[k - 1], recv_sem=small_recv.at[k - 1],
            device_id=others[k - 1], device_id_type=MESH,
        )
        small_copies.append(copy)
    near_copies, far_copies, started = [], [], []
    order = list(range(1, columns)) + [0]
    for k in order:
        place = lax.rem(column + k, columns) * 2 + 1 - side
        copy = pltpu.make_async_remote_copy(
            src_ref=rows(part, place), dst_ref=near_slots.at[k],
            send_sem=near_send.at[k], recv_sem=near_recv.at[k],
            device_id=near, device_id_type=MESH,
        )
        copy.start()
        near_copies.append(copy)
    for copy in small_copies:
        copy.start()
    mine = rows(whole, me)
    for k, arrived in zip(order, near_copies):
        arrived.wait_recv()
        place = lax.rem(column + k, columns) * 2 + side
        total = rows(part, place)[...].astype(jnp.float32) + near_slots[k].astype(jnp.float32)
        if k > 0:
            leaving[k - 1] = total.astype(jnp.bfloat16)
            copy = pltpu.make_async_remote_copy(
                src_ref=leaving.at[k - 1], dst_ref=far_slots.at[k - 1],
                send_sem=far_send.at[k - 1], recv_sem=far_recv.at[k - 1],
                device_id=far[k - 1], device_id_type=MESH,
            )
            copy.start()
            far_copies.append(copy)
    for copy in far_copies:
        copy.wait_recv()
    for k in range(1, columns):
        total = total + far_slots[k - 1].astype(jnp.float32)
    mine[...] = total.astype(jnp.bfloat16)
    for k in range(1, columns):
        copy = pltpu.make_async_remote_copy(
            src_ref=mine, dst_ref=rows(whole, me),
            send_sem=back_send.at[k - 1], recv_sem=back_recv.at[k - 1],
            device_id=far[k - 1], device_id_type=MESH,
        )
        copy.start()
        started.append(copy.wait_send)
    copy = pltpu.make_async_remote_copy(
        src_ref=mine, dst_ref=rows(whole, me),
        send_sem=on_send.at[0], recv_sem=on_recv.at[0],
        device_id=near, device_id_type=MESH,
    )
    copy.start()
    started.append(copy.wait)
    for copy in small_copies:
        copy.wait_recv()
    small_total = small[...]
    for k in range(1, size):
        small_total = small_total + small_slots[k - 1]
    small_sum[...] = small_total
    for k in range(1, columns):
        place = lax.rem(column + columns - k, columns) * 2 + side
        landed = pltpu.make_async_remote_copy(
            src_ref=mine, dst_ref=rows(whole, place),
            send_sem=back_send.at[k - 1], recv_sem=back_recv.at[k - 1],
            device_id=near, device_id_type=MESH,
        )
        landed.wait_recv()
        copy = pltpu.make_async_remote_copy(
            src_ref=rows(whole, place), dst_ref=rows(whole, place),
            send_sem=on_send.at[k], recv_sem=on_recv.at[k],
            device_id=near, device_id_type=MESH,
        )
        copy.start()
        started.append(copy.wait)
    for wait in started:
        wait()
    for copy in near_copies + far_copies + small_copies:
        copy.wait_send()


def total_tensor(part, small, collective_id):
    size = lax.axis_size("tensor")
    columns = size // 2
    length, width = part.shape
    share = length // size
    dma = pltpu.SemaphoreType.DMA
    return pl.pallas_call(
        functools.partial(total_kernel, size),
        out_shape=(
            jax.ShapeDtypeStruct(part.shape, jnp.bfloat16),
            jax.ShapeDtypeStruct(small.shape, jnp.float32),
        ),
        in_specs=[pl.BlockSpec(memory_space=pltpu.VMEM)] * 2,
        out_specs=tuple([pl.BlockSpec(memory_space=pltpu.VMEM)] * 2),
        scratch_shapes=[
            pltpu.VMEM((columns, share, width), jnp.bfloat16),
            pltpu.VMEM((columns - 1, share, width), jnp.bfloat16),
            pltpu.VMEM((columns - 1, share, width), jnp.bfloat16),
            pltpu.VMEM((size - 1,) + small.shape, jnp.float32),
            dma((columns,)),
            dma((columns,)),
            dma((columns - 1,)),
            dma((columns - 1,)),
            dma((columns - 1,)),
            dma((columns - 1,)),
            dma((columns,)),
            dma((columns,)),
            dma((size - 1,)),
            dma((size - 1,)),
        ],
        compiler_params=pltpu.CompilerParams(
            collective_id=collective_id, has_side_effects=True, vmem_limit_bytes=VMEM_BYTES
        ),
    )(part, small)


def pack_rows(rows):
    padded = [jnp.pad(row, (0, 128 - row.shape[0])) for row in rows]
    padded = padded + [jnp.zeros_like(padded[0])] * (16 - len(padded))
    return jnp.stack(padded)


def pack_sums(vectors, size):
    blocks = []
    for vector in vectors:
        share = vector.reshape(size, -1)
        blocks.append(jnp.pad(share, ((0, 0), (0, 128 - share.shape[1]))))
    blocks = blocks + [jnp.zeros_like(blocks[0])] * (16 - len(blocks))
    return jnp.stack(blocks, axis=1).reshape(size * 16, 128).astype(jnp.bfloat16)


def swiglu(gate_in, up_in):
    return jax.nn.silu(gate_in) * up_in


def body(
    tokens,
    cotangent,
    segments,
    positions,
    attn_gain,
    w_query,
    w_key,
    w_value,
    query_gain,
    key_gain,
    w_out,
    ffn_gain,
    w_gate,
    w_up,
    w_down,
):
    dp_size = lax.axis_size("dp")
    gain_tile = pack_rows([attn_gain, ffn_gain, query_gain, key_gain])
    gain_tiles, query_full, key_full, value_full, out_full = gather_dp(
        (gain_tile, w_query, w_key, w_value, w_out.T), 1
    )
    gain_tiles = gain_tiles.reshape(dp_size, 16, 128)
    gain_first = gain_tiles[:, 0, : attn_gain.shape[0]].reshape(-1)
    gain_second = gain_tiles[:, 1, : ffn_gain.shape[0]].reshape(-1)
    qgain_full = gain_tiles[:, 2, : query_gain.shape[0]].reshape(-1)
    kgain_full = gain_tiles[:, 3, : key_gain.shape[0]].reshape(-1)
    no_small = jnp.zeros((8, 128), jnp.float32)
    token_count = tokens.shape[0]
    seq_count = token_count // LEN
    local_heads = query_full.shape[1] // HD
    local_kv = key_full.shape[1] // HD
    group_size = local_heads // local_kv
    share_rows = token_count // lax.axis_size("tensor")
    own_start = lax.axis_index("tensor") * share_rows
    inputs = tokens.astype(jnp.float32)
    attn_scale = gain_first.astype(jnp.float32)
    normed_float, attn_norm_back = jax.vjp(norm_rows, inputs, attn_scale)
    normed = normed_float.astype(jnp.bfloat16)
    query_raw = matmul(normed, query_full).reshape(token_count, local_heads, HD)
    key_raw = matmul(normed, key_full).reshape(token_count, local_kv, HD)
    value_low = (
        matmul(normed, value_full).astype(jnp.bfloat16).reshape(seq_count, LEN, local_kv, HD)
    )
    cosine, sine_table = rope_tables(positions)

    def head_prep(raw_rows, gain_rows):
        return rotate_half(norm_rows(raw_rows, gain_rows), cosine, sine_table)

    query_prep, query_back = jax.vjp(head_prep, query_raw, qgain_full.astype(jnp.float32))
    key_prep, key_back = jax.vjp(head_prep, key_raw, kgain_full.astype(jnp.float32))
    query_low = query_prep.astype(jnp.bfloat16).reshape(seq_count, LEN, local_kv, group_size, HD)
    key_low = key_prep.astype(jnp.bfloat16).reshape(seq_count, LEN, local_kv, HD)
    seq_segments = segments.reshape(seq_count, LEN)
    mixed, lse_rows = lax.map(attend, (query_low, key_low, value_low, seq_segments))
    mixed_low = mixed.reshape(token_count, local_heads * HD).astype(jnp.bfloat16)
    attn_part = matmul_nt(mixed_low, out_full).astype(jnp.bfloat16)
    gate_full, up_full, down_full = gather_dp((w_gate, w_up, w_down.T), 2)
    ffn_scale = gain_second.astype(jnp.float32)
    attn_total, _ = total_tensor(attn_part, no_small, 3)
    residual = inputs + attn_total.astype(jnp.float32)
    ffn_float, ffn_norm_back = jax.vjp(norm_rows, residual, ffn_scale)
    normed_ffn = ffn_float.astype(jnp.bfloat16)
    residual_rows = lax.dynamic_slice_in_dim(residual, own_start, share_rows, 0)
    gate_value = matmul(normed_ffn, gate_full)
    up_value = matmul(normed_ffn, up_full)
    hidden_float, swiglu_back = jax.vjp(swiglu, gate_value, up_value)
    hidden = hidden_float.astype(jnp.bfloat16)
    ffn_share = lax.psum_scatter(
        matmul_nt(
            lax.slice_in_dim(hidden, 0, share_rows * lax.axis_size("tensor"), axis=0), down_full
        ).astype(jnp.bfloat16),
        "tensor",
        scatter_dimension=0,
        tiled=True,
    ).astype(jnp.float32)
    output = (residual_rows + ffn_share).astype(jnp.bfloat16)
    grad_output = cotangent.astype(jnp.float32)
    down_grad = matmul_tn(cotangent, hidden)
    grad_hidden = matmul(cotangent, down_full)
    grad_gate, grad_up = swiglu_back(grad_hidden)
    gate_low = grad_gate.astype(jnp.bfloat16)
    up_low = grad_up.astype(jnp.bfloat16)
    gate_grad = matmul_tn(normed_ffn, gate_low)
    up_grad = matmul_tn(normed_ffn, up_low)
    ffn_input_part = matmul_nt(gate_low, gate_full) + matmul_nt(up_low, up_full)
    ffn_input_grad, _ = total_tensor(ffn_input_part.astype(jnp.bfloat16), no_small, 4)
    residual_part, ffn_gain_part = ffn_norm_back(ffn_input_grad.astype(jnp.float32))
    grad_residual = residual_part + grad_output
    grad_attn_low = grad_residual.astype(jnp.bfloat16)
    out_grad = matmul_tn(grad_attn_low, mixed_low)
    grad_mixed = (
        matmul(grad_attn_low, out_full)
        .astype(jnp.bfloat16)
        .reshape(seq_count, LEN, local_kv, group_size, HD)
    )
    grad_query, grad_key, grad_value = lax.map(
        attend_back, (query_low, key_low, value_low, seq_segments, lse_rows, grad_mixed)
    )
    grad_qraw, grad_qgain = query_back(grad_query.reshape(token_count, local_heads, HD))
    grad_kraw, grad_kgain = key_back(grad_key.reshape(token_count, local_kv, HD))
    query_low_grad = grad_qraw.reshape(token_count, local_heads * HD).astype(jnp.bfloat16)
    key_low_grad = grad_kraw.reshape(token_count, local_kv * HD).astype(jnp.bfloat16)
    value_low_grad = grad_value.reshape(token_count, local_kv * HD).astype(jnp.bfloat16)
    query_weight_grad = matmul_tn(normed, query_low_grad)
    key_weight_grad = matmul_tn(normed, key_low_grad)
    value_weight_grad = matmul_tn(normed, value_low_grad)
    attn_input_part = (
        matmul_nt(query_low_grad, query_full)
        + matmul_nt(key_low_grad, key_full)
        + matmul_nt(value_low_grad, value_full)
    )
    gain_sums = jnp.pad(
        jnp.stack([grad_qgain, grad_kgain]), ((0, 6), (0, 128 - grad_qgain.shape[0]))
    )
    attn_input_grad, gain_sums = total_tensor(attn_input_part.astype(jnp.bfloat16), gain_sums, 5)
    qgain_total = gain_sums[0, : grad_qgain.shape[0]]
    kgain_total = gain_sums[1, : grad_kgain.shape[0]]
    input_part, attn_gain_grad = attn_norm_back(attn_input_grad.astype(jnp.float32))
    tokens_grad = input_part + grad_residual
    ffn_grads = scatter_dp(
        [grad.astype(jnp.bfloat16) for grad in (gate_grad, up_grad, down_grad)], 6
    )
    gain_grads = pack_sums([attn_gain_grad, ffn_gain_part, qgain_total, kgain_total], dp_size)
    attn_grads = scatter_dp(
        [gain_grads]
        + [
            grad.astype(jnp.bfloat16)
            for grad in (query_weight_grad, key_weight_grad, value_weight_grad, out_grad)
        ],
        7,
    )
    gain_grads = attn_grads[0]
    return (
        output,
        tokens_grad,
        gain_grads[0, : attn_gain.shape[0]],
        attn_grads[1],
        attn_grads[2],
        attn_grads[3],
        gain_grads[2, : query_gain.shape[0]],
        gain_grads[3, : key_gain.shape[0]],
        attn_grads[4].T,
        gain_grads[1, : ffn_gain.shape[0]],
        ffn_grads[0],
        ffn_grads[1],
        ffn_grads[2].T,
    )


def solution(mesh):
    placed = (
        P("dp", None),
        P("dp", None),
        P("dp"),
        P("dp"),
        P("dp"),
        P("dp", "tensor"),
        P("dp", "tensor"),
        P("dp", "tensor"),
        P("dp"),
        P("dp"),
        P("tensor", "dp"),
        P("dp"),
        P("dp", "tensor"),
        P("dp", "tensor"),
        P("tensor", "dp"),
    )
    return jax.shard_map(
        body,
        mesh=mesh,
        in_specs=placed,
        out_specs=(
            P(("dp", "tensor"), None),
            P("dp", None),
            P("dp"),
            P("dp", "tensor"),
            P("dp", "tensor"),
            P("dp", "tensor"),
            P("dp"),
            P("dp"),
            P("tensor", "dp"),
            P("dp"),
            P("dp", "tensor"),
            P("dp", "tensor"),
            P("tensor", "dp"),
        ),
        check_vma=False,
    )
```

```python
import functools

import jax
import jax.numpy as jnp
from jax import lax
from jax.experimental import pallas as pl
from jax.experimental.pallas import tpu as pltpu
from jax.sharding import PartitionSpec as P

HD = 64
LEN = 1024


EPSILON = 1e-05
ROPE_BASE = 1000000.0
MASKED = -1e30


def norm_rows(values, gain):
    return values * lax.rsqrt(jnp.mean(values * values, axis=-1, keepdims=True) + EPSILON) * gain


def rotate_half(values, cosine, sine_table):
    halfway = values.shape[-1] // 2
    first_half = values[..., :halfway]
    second_half = values[..., halfway:]
    return jnp.concatenate(
        [
            first_half * cosine - second_half * sine_table,
            second_half * cosine + first_half * sine_table,
        ],
        axis=-1,
    )


def rope_tables(positions):
    halfway = HD // 2
    frequency = ROPE_BASE ** (-(jnp.arange(halfway, dtype=jnp.float32) * 2.0 / HD))
    angle_grid = positions.astype(jnp.float32)[:, None] * frequency[None, :]
    return (jnp.cos(angle_grid)[:, None, :], jnp.sin(angle_grid)[:, None, :])


def matmul(left, right):
    return jnp.dot(left, right, preferred_element_type=jnp.float32)


def matmul_tn(left, right):
    return lax.dot_general(
        left, right, (((0,), (0,)), ((), ())), preferred_element_type=jnp.float32
    )


def matmul_nt(left, right):
    return lax.dot_general(
        left, right, (((1,), (1,)), ((), ())), preferred_element_type=jnp.float32
    )


def block_scores(query_block, key_rows, seq_segments, first_row, last_row):
    score_scale = query_block.shape[-1] ** (-0.5)
    places = jnp.arange(seq_segments.shape[0])
    scores = (
        jnp.einsum("tkgd,skd->kgts", query_block, key_rows, preferred_element_type=jnp.float32)
        * score_scale
    )
    allowed = (places[first_row:last_row, None] >= places[None, :last_row]) & (
        seq_segments[first_row:last_row, None] == seq_segments[None, :last_row]
    )
    return jnp.where(allowed, scores, MASKED)


def attend(operands):
    queries, keys_low, values_low, seq_segments = operands
    length = queries.shape[0]
    block_rows = min(512, length)
    pieces = []
    lse_parts = []
    for first_row in range(0, length, block_rows):
        last_row = first_row + block_rows
        scores = block_scores(
            queries[first_row:last_row], keys_low[:last_row], seq_segments, first_row, last_row
        )
        row_max = jnp.max(scores, axis=-1, keepdims=True)
        shifted = jnp.exp(scores - row_max)
        totals = jnp.sum(shifted, axis=-1, keepdims=True)
        probabilities = (shifted / totals).astype(jnp.bfloat16)
        pieces.append(
            jnp.einsum(
                "kgts,skd->tkgd",
                probabilities,
                values_low[:last_row],
                preferred_element_type=jnp.float32,
            )
        )
        lse_parts.append(row_max + jnp.log(totals))
    return (jnp.concatenate(pieces, axis=0), jnp.concatenate(lse_parts, axis=2))


def attend_back(operands, between):
    queries, keys_low, values_low, seq_segments, lse_rows, grad_mixed = operands
    length = queries.shape[0]
    block_rows = min(512, length)
    score_scale = queries.shape[-1] ** (-0.5)
    key_total = jnp.zeros(keys_low.shape, jnp.float32)
    value_total = jnp.zeros(values_low.shape, jnp.float32)
    query_pieces = []
    for first_row in reversed(range(0, length, block_rows)):
        if first_row == 0:
            key_total, value_total, grad_mixed, *between = lax.optimization_barrier(
                (key_total, value_total, grad_mixed, *between)
            )
        last_row = first_row + block_rows
        scores = block_scores(
            queries[first_row:last_row], keys_low[:last_row], seq_segments, first_row, last_row
        )
        probabilities = jnp.exp(scores - lse_rows[:, :, first_row:last_row])
        grad_block = grad_mixed[first_row:last_row]
        grad_probs = jnp.einsum(
            "tkgd,skd->kgts", grad_block, values_low[:last_row], preferred_element_type=jnp.float32
        )
        row_terms = jnp.sum(probabilities * grad_probs, axis=-1, keepdims=True)
        grad_scores = (probabilities * (grad_probs - row_terms)).astype(jnp.bfloat16)
        query_pieces.append(
            jnp.einsum(
                "kgts,skd->tkgd",
                grad_scores,
                keys_low[:last_row],
                preferred_element_type=jnp.float32,
            )
            * score_scale
        )
        padding = ((0, length - last_row), (0, 0), (0, 0))
        key_part = (
            jnp.einsum(
                "kgts,tkgd->skd",
                grad_scores,
                queries[first_row:last_row],
                preferred_element_type=jnp.float32,
            )
            * score_scale
        )
        value_part = jnp.einsum(
            "kgts,tkgd->skd",
            probabilities.astype(jnp.bfloat16),
            grad_block,
            preferred_element_type=jnp.float32,
        )
        key_total = key_total + jnp.pad(key_part, padding)
        value_total = value_total + jnp.pad(value_part, padding)
    return (jnp.concatenate(query_pieces[::-1], axis=0), key_total, value_total, between)


MESH = pl.DeviceIdType.MESH
VMEM_BYTES = 44 * 1024 * 1024


def block_of(ref, place, size):
    return ref.at[pl.ds(pl.multiple_of(place * size, size), size), :]


def greet(peers):
    barrier = pltpu.get_barrier_semaphore()
    for peer in peers:
        pl.semaphore_signal(barrier, inc=1, device_id=peer, device_id_type=MESH)
    pl.semaphore_wait(barrier, len(peers))


def dp_places(size):
    me = lax.axis_index("dp")
    return me // 2, lax.rem(me, 2), size // 2


def gather_kernel(size, count, *refs):
    shards, wholes = refs[:count], refs[count : 2 * count]
    own_sem, far_send, far_recv, near_send, near_recv = refs[2 * count :]
    column, side, columns = dp_places(size)
    near = {"dp": column * 2 + 1 - side}
    far = [{"dp": lax.rem(column + k, columns) * 2 + side} for k in range(1, columns)]
    greet([near] + far)
    mine = column * 2 + side
    started = []

    def slot(a, place):
        return block_of(wholes[a], place, shards[a].shape[0])

    for a in range(count):
        own = pltpu.make_async_copy(shards[a], slot(a, mine), own_sem.at[a])
        own.start()
        started.append(own.wait)
        copy = pltpu.make_async_remote_copy(
            src_ref=shards[a], dst_ref=slot(a, mine),
            send_sem=near_send.at[a, 0], recv_sem=near_recv.at[a, 0],
            device_id=near, device_id_type=MESH,
        )
        copy.start()
        started.append(copy.wait)
    arrivals = []
    for k in range(1, columns):
        for a in range(count):
            copy = pltpu.make_async_remote_copy(
                src_ref=shards[a], dst_ref=slot(a, mine),
                send_sem=far_send.at[a, k - 1], recv_sem=far_recv.at[a, k - 1],
                device_id=far[k - 1], device_id_type=MESH,
            )
            copy.start()
            started.append(copy.wait_send)
            arrivals.append((k, a))
    for k, a in arrivals:
        place = lax.rem(column + columns - k, columns) * 2 + side
        landed = pltpu.make_async_remote_copy(
            src_ref=shards[a], dst_ref=slot(a, place),
            send_sem=far_send.at[a, k - 1], recv_sem=far_recv.at[a, k - 1],
            device_id=near, device_id_type=MESH,
        )
        landed.wait_recv()
        copy = pltpu.make_async_remote_copy(
            src_ref=slot(a, place), dst_ref=slot(a, place),
            send_sem=near_send.at[a, k], recv_sem=near_recv.at[a, k],
            device_id=near, device_id_type=MESH,
        )
        copy.start()
        started.append(copy.wait)
    for wait in started:
        wait()


def gather_dp(arrays, collective_id):
    size = lax.axis_size("dp")
    columns, count = size // 2, len(arrays)
    shapes = [
        jax.ShapeDtypeStruct((size * array.shape[0], array.shape[1]), array.dtype)
        for array in arrays
    ]
    dma = pltpu.SemaphoreType.DMA
    return pl.pallas_call(
        functools.partial(gather_kernel, size, count),
        out_shape=tuple(shapes),
        in_specs=[pl.BlockSpec(memory_space=pl.ANY)] * count,
        out_specs=tuple([pl.BlockSpec(memory_space=pl.ANY)] * count),
        scratch_shapes=[
            dma((count,)),
            dma((count, columns - 1)),
            dma((count, columns - 1)),
            dma((count, columns)),
            dma((count, columns)),
        ],
        compiler_params=pltpu.CompilerParams(collective_id=collective_id, has_side_effects=True),
        cost_estimate=pl.CostEstimate(flops=0, bytes_accessed=80_000_000, transcendentals=0),
    )(*arrays)


def scatter_kernel(size, count, later, *refs):
    parts, refs = refs[:count], refs[later:]
    sums = refs[count : 2 * count]
    near_slots = refs[2 * count : 3 * count]
    leaving = refs[3 * count : 4 * count]
    far_slots = refs[4 * count : 5 * count]
    near_send, near_recv, far_send, far_recv = refs[5 * count :]
    column, side, columns = dp_places(size)
    near = {"dp": column * 2 + 1 - side}
    far = [{"dp": lax.rem(column + k, columns) * 2 + side} for k in range(1, columns)]
    greet([near] + far)
    order = [(k, a) for k in list(range(1, columns)) + [0] for a in range(count)]

    def part(a, place):
        return block_of(parts[a], place, sums[a].shape[0])

    near_copies, far_copies = {}, {}
    for k, a in order:
        place = lax.rem(column + k, columns) * 2 + 1 - side
        copy = pltpu.make_async_remote_copy(
            src_ref=part(a, place), dst_ref=near_slots[a].at[k],
            send_sem=near_send.at[a, k], recv_sem=near_recv.at[a, k],
            device_id=near, device_id_type=MESH,
        )
        copy.start()
        near_copies[k, a] = copy
    for k, a in order:
        near_copies[k, a].wait_recv()
        place = lax.rem(column + k, columns) * 2 + side
        total = part(a, place)[...].astype(jnp.float32) + near_slots[a][k].astype(jnp.float32)
        if k == 0:
            sums[a][...] = total
            continue
        leaving[a][k - 1] = total.astype(jnp.bfloat16)
        copy = pltpu.make_async_remote_copy(
            src_ref=leaving[a].at[k - 1], dst_ref=far_slots[a].at[k - 1],
            send_sem=far_send.at[a, k - 1], recv_sem=far_recv.at[a, k - 1],
            device_id=far[k - 1], device_id_type=MESH,
        )
        copy.start()
        far_copies[k, a] = copy
    for k, a in order:
        if k > 0:
            far_copies[k, a].wait_recv()
            sums[a][...] += far_slots[a][k - 1].astype(jnp.float32)
    for k, a in order:
        near_copies[k, a].wait_send()
        if k > 0:
            far_copies[k, a].wait_send()


def scatter_dp(arrays, after, collective_id):
    size = lax.axis_size("dp")
    columns, count = size // 2, len(arrays)
    shapes = [(array.shape[0] // size, array.shape[1]) for array in arrays]
    dma = pltpu.SemaphoreType.DMA
    return pl.pallas_call(
        functools.partial(scatter_kernel, size, count, len(after)),
        out_shape=tuple(jax.ShapeDtypeStruct(shape, jnp.float32) for shape in shapes),
        in_specs=[pl.BlockSpec(memory_space=pltpu.VMEM)] * count
        + [pl.BlockSpec(memory_space=pl.ANY)] * len(after),
        out_specs=tuple([pl.BlockSpec(memory_space=pltpu.VMEM)] * count),
        scratch_shapes=[pltpu.VMEM((columns,) + shape, jnp.bfloat16) for shape in shapes]
        + [pltpu.VMEM((columns - 1,) + shape, jnp.bfloat16) for shape in shapes]
        + [pltpu.VMEM((columns - 1,) + shape, jnp.bfloat16) for shape in shapes]
        + [
            dma((count, columns)),
            dma((count, columns)),
            dma((count, columns - 1)),
            dma((count, columns - 1)),
        ],
        compiler_params=pltpu.CompilerParams(
            collective_id=collective_id, has_side_effects=True, vmem_limit_bytes=VMEM_BYTES
        ),
        cost_estimate=pl.CostEstimate(flops=0, bytes_accessed=80_000_000, transcendentals=0),
    )(*arrays, *after)


def total_kernel(size, dp_size, later, swaps, *refs):
    part, small, whole, small_sum = refs[0], refs[1], refs[2 + later], refs[3 + later]
    parts, swapped = refs[2 : 2 + later], refs[4 + later]
    swap_send, swap_recv = refs[-2:]
    (near_slots, leaving, far_slots, small_slots, near_send, near_recv, far_send, far_recv,
     back_send, back_recv, on_send, on_recv, small_send, small_recv) = refs[5 + later : -2]
    me = lax.axis_index("tensor")
    column, side, columns = me // 2, lax.rem(me, 2), size // 2
    share = whole.shape[0] // size
    near = {"tensor": column * 2 + 1 - side}
    far = [{"tensor": lax.rem(column + k, columns) * 2 + side} for k in range(1, columns)]
    others = [{"tensor": lax.rem(me + k, size)} for k in range(1, size)]
    dp_column, dp_side, dp_columns = dp_places(dp_size)
    twin = {"dp": dp_column * 2 + 1 - dp_side}
    greet(others + [twin] if swaps else others)

    def rows(ref, place):
        return block_of(ref, place, share)

    small_copies = []
    for k in range(1, size):
        copy = pltpu.make_async_remote_copy(
            src_ref=small, dst_ref=small_slots.at[k - 1],
            send_sem=small_send.at[k - 1], recv_sem=small_recv.at[k - 1],
            device_id=others[k - 1], device_id_type=MESH,
        )
        small_copies.append(copy)
    near_copies, far_copies, started = [], [], []
    order = list(range(1, columns)) + [0]
    for k in order:
        place = lax.rem(column + k, columns) * 2 + 1 - side
        copy = pltpu.make_async_remote_copy(
            src_ref=rows(part, place), dst_ref=near_slots.at[k],
            send_sem=near_send.at[k], recv_sem=near_recv.at[k],
            device_id=near, device_id_type=MESH,
        )
        copy.start()
        near_copies.append(copy)
    for copy in small_copies:
        copy.start()
    for step in range(1, swaps + 1):
        place = lax.rem(dp_column + step, dp_columns) * 2 + 1 - dp_side
        for a in range(later):
            rows_each = parts[a].shape[0] // dp_size
            copy = pltpu.make_async_remote_copy(
                src_ref=block_of(parts[a], place, rows_each),
                dst_ref=swapped.at[step - 1, pl.ds(a * rows_each, rows_each), :],
                send_sem=swap_send.at[step - 1, a], recv_sem=swap_recv.at[step - 1, a],
                device_id=twin, device_id_type=MESH,
            )
            copy.start()
            started.append(copy.wait)
    mine = rows(whole, me)
    for k, arrived in zip(order, near_copies):
        arrived.wait_recv()
        place = lax.rem(column + k, columns) * 2 + side
        total = rows(part, place)[...].astype(jnp.float32) + near_slots[k].astype(jnp.float32)
        if k > 0:
            leaving[k - 1] = total.astype(jnp.bfloat16)
            copy = pltpu.make_async_remote_copy(
                src_ref=leaving.at[k - 1], dst_ref=far_slots.at[k - 1],
                send_sem=far_send.at[k - 1], recv_sem=far_recv.at[k - 1],
                device_id=far[k - 1], device_id_type=MESH,
            )
            copy.start()
            far_copies.append(copy)
    for copy in far_copies:
        copy.wait_recv()
    for k in range(1, columns):
        total = total + far_slots[k - 1].astype(jnp.float32)
    mine[...] = total.astype(jnp.bfloat16)
    for k in range(1, columns):
        copy = pltpu.make_async_remote_copy(
            src_ref=mine, dst_ref=rows(whole, me),
            send_sem=back_send.at[k - 1], recv_sem=back_recv.at[k - 1],
            device_id=far[k - 1], device_id_type=MESH,
        )
        copy.start()
        started.append(copy.wait_send)
    copy = pltpu.make_async_remote_copy(
        src_ref=mine, dst_ref=rows(whole, me),
        send_sem=on_send.at[0], recv_sem=on_recv.at[0],
        device_id=near, device_id_type=MESH,
    )
    copy.start()
    started.append(copy.wait)
    for copy in small_copies:
        copy.wait_recv()
    small_total = small[...]
    for k in range(1, size):
        small_total = small_total + small_slots[k - 1]
    small_sum[...] = small_total
    for k in range(1, columns):
        place = lax.rem(column + columns - k, columns) * 2 + side
        landed = pltpu.make_async_remote_copy(
            src_ref=mine, dst_ref=rows(whole, place),
            send_sem=back_send.at[k - 1], recv_sem=back_recv.at[k - 1],
            device_id=near, device_id_type=MESH,
        )
        landed.wait_recv()
        copy = pltpu.make_async_remote_copy(
            src_ref=rows(whole, place), dst_ref=rows(whole, place),
            send_sem=on_send.at[k], recv_sem=on_recv.at[k],
            device_id=near, device_id_type=MESH,
        )
        copy.start()
        started.append(copy.wait)
    for wait in started:
        wait()
    for copy in near_copies + far_copies + small_copies:
        copy.wait_send()


def total_tensor(part, small, after, swaps, collective_id):
    size = lax.axis_size("tensor")
    columns = size // 2
    length, width = part.shape
    share = length // size
    dp_size = lax.axis_size("dp")
    if swaps:
        rows = len(after) * after[0].shape[0] // dp_size
        swapped = jax.ShapeDtypeStruct((swaps, rows, after[0].shape[1]), jnp.bfloat16)
    else:
        swapped = jax.ShapeDtypeStruct((1, 16, 128), jnp.bfloat16)
    dma = pltpu.SemaphoreType.DMA
    return pl.pallas_call(
        functools.partial(total_kernel, size, dp_size, len(after), swaps),
        out_shape=(
            jax.ShapeDtypeStruct(part.shape, jnp.bfloat16),
            jax.ShapeDtypeStruct(small.shape, jnp.float32),
            swapped,
        ),
        in_specs=[pl.BlockSpec(memory_space=pltpu.VMEM)] * 2
        + [pl.BlockSpec(memory_space=pl.ANY)] * len(after),
        out_specs=tuple([pl.BlockSpec(memory_space=pltpu.VMEM)] * 2)
        + (pl.BlockSpec(memory_space=pl.ANY),),
        scratch_shapes=[
            pltpu.VMEM((columns, share, width), jnp.bfloat16),
            pltpu.VMEM((columns - 1, share, width), jnp.bfloat16),
            pltpu.VMEM((columns - 1, share, width), jnp.bfloat16),
            pltpu.VMEM((size - 1,) + small.shape, jnp.float32),
            dma((columns,)),
            dma((columns,)),
            dma((columns - 1,)),
            dma((columns - 1,)),
            dma((columns - 1,)),
            dma((columns - 1,)),
            dma((columns,)),
            dma((columns,)),
            dma((size - 1,)),
            dma((size - 1,)),
            dma((max(swaps, 1), max(len(after), 1))),
            dma((max(swaps, 1), max(len(after), 1))),
        ],
        compiler_params=pltpu.CompilerParams(
            collective_id=collective_id, has_side_effects=True, vmem_limit_bytes=VMEM_BYTES
        ),
        cost_estimate=pl.CostEstimate(flops=0, bytes_accessed=80_000_000, transcendentals=0),
    )(part, small, *after)


def shifted_pairs(size, step):
    return [(place, (place + 2 * step) % size) for place in range(size)]


def swapped_pairs(size):
    return [(place, place ^ 1) for place in range(size)]


def gather_start(shard):
    size = lax.axis_size("dp")
    columns = size // 2
    middle = columns // 2
    blocks = {0: shard}
    for step in range(1, columns):
        if step != middle:
            blocks[step] = lax.ppermute(shard, "dp", shifted_pairs(size, step))
    first = [step for step in blocks if step > 0]
    held, *came = lax.optimization_barrier((shard, *[blocks[step] for step in first]))
    blocks.update(zip(first, came))
    blocks[middle] = lax.ppermute(held, "dp", shifted_pairs(size, middle))
    return [blocks[step] for step in range(columns)], came


def gather_end(blocks, twins, count):
    size = lax.axis_size("dp")
    column, side, columns = dp_places(size)
    rows = blocks[0].shape[0] // count
    wholes = []
    for a in range(count):
        whole = jnp.zeros((size * rows, blocks[0].shape[1]), blocks[0].dtype)
        for step in range(columns):
            base = lax.rem(column + columns - step, columns) * 2
            for held, place in ((blocks[step], base + side), (twins[step], base + 1 - side)):
                whole = lax.dynamic_update_slice_in_dim(
                    whole, held[a * rows : (a + 1) * rows], place * rows, 0
                )
        wholes.append(whole)
    return wholes


def swap_sides(block):
    return lax.ppermute(block, "dp", swapped_pairs(lax.axis_size("dp")))


def scatter_start(parts, swapped):
    size = lax.axis_size("dp")
    column, side, columns = dp_places(size)
    rows = parts[0].shape[0] // size

    def blocks_for(place):
        return jnp.concatenate(
            [lax.dynamic_slice_in_dim(part, place * rows, rows, 0) for part in parts], axis=0
        )

    sums = []
    for step in list(range(1, columns)) + [0]:
        base = lax.rem(column + step, columns) * 2
        if 0 < step <= swapped.shape[0]:
            came = swapped[step - 1]
        else:
            came = swap_sides(blocks_for(base + 1 - side))
        both = blocks_for(base + side).astype(jnp.float32) + came.astype(jnp.float32)
        sums.append(both.astype(jnp.bfloat16))
    return sums


def scatter_step(block, step):
    return lax.ppermute(block, "dp", shifted_pairs(lax.axis_size("dp"), step))


def pack_rows(rows):
    padded = [jnp.pad(row, (0, 128 - row.shape[0])) for row in rows]
    padded = padded + [jnp.zeros_like(padded[0])] * (16 - len(padded))
    return jnp.stack(padded)


def pack_sums(vectors, size):
    blocks = []
    for vector in vectors:
        share = vector.reshape(size, -1)
        blocks.append(jnp.pad(share, ((0, 0), (0, 128 - share.shape[1]))))
    blocks = blocks + [jnp.zeros_like(blocks[0])] * (16 - len(blocks))
    return jnp.stack(blocks, axis=1).reshape(size * 16, 128).astype(jnp.bfloat16)


def swiglu(gate_in, up_in):
    return jax.nn.silu(gate_in) * up_in


def body(
    tokens,
    cotangent,
    segments,
    positions,
    attn_gain,
    w_query,
    w_key,
    w_value,
    query_gain,
    key_gain,
    w_out,
    ffn_gain,
    w_gate,
    w_up,
    w_down,
):
    dp_size = lax.axis_size("dp")
    gain_tile = pack_rows([attn_gain, ffn_gain, query_gain, key_gain])
    gain_tiles, query_full, key_full, value_full, out_full = gather_dp(
        (gain_tile, w_query, w_key, w_value, w_out.T), 1
    )
    gain_tiles, *ffn_shards = lax.optimization_barrier((gain_tiles, w_gate, w_up, w_down.T))
    ffn_shard = jnp.concatenate(ffn_shards, axis=0)
    columns = dp_size // 2
    ffn_blocks, ffn_first = gather_start(ffn_shard)
    ffn_twins = [swap_sides(ffn_shard)]
    gain_tiles = gain_tiles.reshape(dp_size, 16, 128)
    gain_first = gain_tiles[:, 0, : attn_gain.shape[0]].reshape(-1)
    gain_second = gain_tiles[:, 1, : ffn_gain.shape[0]].reshape(-1)
    qgain_full = gain_tiles[:, 2, : query_gain.shape[0]].reshape(-1)
    kgain_full = gain_tiles[:, 3, : key_gain.shape[0]].reshape(-1)
    no_small = jnp.zeros((8, 128), jnp.float32)
    token_count = tokens.shape[0]
    seq_count = token_count // LEN
    local_heads = query_full.shape[1] // HD
    local_kv = key_full.shape[1] // HD
    group_size = local_heads // local_kv
    share_rows = token_count // lax.axis_size("tensor")
    own_start = lax.axis_index("tensor") * share_rows
    inputs = tokens.astype(jnp.float32)
    attn_scale = gain_first.astype(jnp.float32)
    normed_float, attn_norm_back = jax.vjp(norm_rows, inputs, attn_scale)
    normed = normed_float.astype(jnp.bfloat16)
    query_raw = matmul(normed, query_full).reshape(token_count, local_heads, HD)
    key_raw = matmul(normed, key_full).reshape(token_count, local_kv, HD)
    value_low = (
        matmul(normed, value_full).astype(jnp.bfloat16).reshape(seq_count, LEN, local_kv, HD)
    )
    cosine, sine_table = rope_tables(positions)

    def head_prep(raw_rows, gain_rows):
        return rotate_half(norm_rows(raw_rows, gain_rows), cosine, sine_table)

    query_prep, query_back = jax.vjp(head_prep, query_raw, qgain_full.astype(jnp.float32))
    key_prep, key_back = jax.vjp(head_prep, key_raw, kgain_full.astype(jnp.float32))
    query_low = query_prep.astype(jnp.bfloat16).reshape(seq_count, LEN, local_kv, group_size, HD)
    key_low = key_prep.astype(jnp.bfloat16).reshape(seq_count, LEN, local_kv, HD)
    seq_segments = segments.reshape(seq_count, LEN)
    mixed, lse_rows = lax.map(attend, (query_low, key_low, value_low, seq_segments))
    mixed_low = mixed.reshape(token_count, local_heads * HD).astype(jnp.bfloat16)
    attn_part = matmul_nt(mixed_low, out_full).astype(jnp.bfloat16)
    ffn_scale = gain_second.astype(jnp.float32)
    attn_total, _, _ = total_tensor(attn_part, no_small, ffn_first, 0, 3)
    ffn_twins += [swap_sides(block) for block in ffn_blocks[1:]]
    gate_full, up_full, down_full = gather_end(ffn_blocks, ffn_twins, 3)
    residual = inputs + attn_total.astype(jnp.float32)
    ffn_float, ffn_norm_back = jax.vjp(norm_rows, residual, ffn_scale)
    normed_ffn = ffn_float.astype(jnp.bfloat16)
    residual_rows = lax.dynamic_slice_in_dim(residual, own_start, share_rows, 0)
    gate_value = matmul(normed_ffn, gate_full)
    up_value = matmul(normed_ffn, up_full)
    hidden_float, swiglu_back = jax.vjp(swiglu, gate_value, up_value)
    hidden = hidden_float.astype(jnp.bfloat16)
    ffn_share = lax.psum_scatter(
        matmul_nt(
            lax.slice_in_dim(hidden, 0, share_rows * lax.axis_size("tensor"), axis=0), down_full
        ).astype(jnp.bfloat16),
        "tensor",
        scatter_dimension=0,
        tiled=True,
    ).astype(jnp.float32)
    output = (residual_rows + ffn_share).astype(jnp.bfloat16)
    grad_output = cotangent.astype(jnp.float32)
    down_grad = matmul_tn(cotangent, hidden)
    grad_hidden = matmul(cotangent, down_full)
    grad_gate, grad_up = swiglu_back(grad_hidden)
    gate_low = grad_gate.astype(jnp.bfloat16)
    up_low = grad_up.astype(jnp.bfloat16)
    gate_grad = matmul_tn(normed_ffn, gate_low)
    up_grad = matmul_tn(normed_ffn, up_low)
    ffn_input_part = matmul_nt(gate_low, gate_full) + matmul_nt(up_low, up_full)
    ffn_parts = [grad.astype(jnp.bfloat16) for grad in (gate_grad, up_grad, down_grad)]
    early = min(2, columns - 1)
    ffn_input_grad, _, ffn_swapped = total_tensor(
        ffn_input_part.astype(jnp.bfloat16), no_small, ffn_parts, early, 4
    )
    ffn_sums = scatter_start(ffn_parts, ffn_swapped)
    residual_part, ffn_gain_part = ffn_norm_back(ffn_input_grad.astype(jnp.float32))
    grad_residual = residual_part + grad_output
    grad_attn_low = grad_residual.astype(jnp.bfloat16)
    out_grad = matmul_tn(grad_attn_low, mixed_low)
    grad_mixed = (
        matmul(grad_attn_low, out_full)
        .astype(jnp.bfloat16)
        .reshape(seq_count, LEN, local_kv, group_size, HD)
    )
    ffn_came = {step: scatter_step(ffn_sums[step - 1], step) for step in range(1, early + 1)}
    between = [ffn_came[1]] + ffn_sums[early : columns - 1]
    pieces = []
    for seq in range(seq_count):
        *piece, between = attend_back(
            [
                array[seq]
                for array in (query_low, key_low, value_low, seq_segments, lse_rows, grad_mixed)
            ],
            between,
        )
        pieces.append(piece)
    grad_query, grad_key, grad_value = (jnp.stack(piece) for piece in zip(*pieces))
    ffn_came[1] = between[0]
    for step in range(early + 1, columns):
        ffn_came[step] = scatter_step(between[step - early], step)
    ffn_came = [ffn_came[step] for step in range(1, columns)]
    grad_qraw, grad_qgain = query_back(grad_query.reshape(token_count, local_heads, HD))
    grad_kraw, grad_kgain = key_back(grad_key.reshape(token_count, local_kv, HD))
    query_low_grad = grad_qraw.reshape(token_count, local_heads * HD).astype(jnp.bfloat16)
    key_low_grad = grad_kraw.reshape(token_count, local_kv * HD).astype(jnp.bfloat16)
    value_low_grad = grad_value.reshape(token_count, local_kv * HD).astype(jnp.bfloat16)
    query_weight_grad = matmul_tn(normed, query_low_grad)
    key_weight_grad = matmul_tn(normed, key_low_grad)
    value_weight_grad = matmul_tn(normed, value_low_grad)
    attn_input_part = (
        matmul_nt(query_low_grad, query_full)
        + matmul_nt(key_low_grad, key_full)
        + matmul_nt(value_low_grad, value_full)
    )
    gain_sums = jnp.pad(
        jnp.stack([grad_qgain, grad_kgain]), ((0, 6), (0, 128 - grad_qgain.shape[0]))
    )
    attn_input_grad, gain_sums, _ = total_tensor(
        attn_input_part.astype(jnp.bfloat16), gain_sums, [], 0, 5
    )
    qgain_total = gain_sums[0, : grad_qgain.shape[0]]
    kgain_total = gain_sums[1, : grad_kgain.shape[0]]
    input_part, attn_gain_grad = attn_norm_back(attn_input_grad.astype(jnp.float32))
    tokens_grad = input_part + grad_residual
    ffn_total = ffn_sums[-1].astype(jnp.float32)
    for block in ffn_came:
        ffn_total = ffn_total + block.astype(jnp.float32)
    ffn_grads = jnp.split(ffn_total, 3)
    gain_grads = pack_sums([attn_gain_grad, ffn_gain_part, qgain_total, kgain_total], dp_size)
    attn_grads = scatter_dp(
        [gain_grads]
        + [
            grad.astype(jnp.bfloat16)
            for grad in (query_weight_grad, key_weight_grad, value_weight_grad, out_grad)
        ],
        ffn_came[1:] + ffn_sums[columns - 1 :],
        7,
    )
    gain_grads = attn_grads[0]
    return (
        output,
        tokens_grad,
        gain_grads[0, : attn_gain.shape[0]],
        attn_grads[1],
        attn_grads[2],
        attn_grads[3],
        gain_grads[2, : query_gain.shape[0]],
        gain_grads[3, : key_gain.shape[0]],
        attn_grads[4].T,
        gain_grads[1, : ffn_gain.shape[0]],
        ffn_grads[0],
        ffn_grads[1],
        ffn_grads[2].T,
    )


def solution(mesh):
    placed = (
        P("dp", None),
        P("dp", None),
        P("dp"),
        P("dp"),
        P("dp"),
        P("dp", "tensor"),
        P("dp", "tensor"),
        P("dp", "tensor"),
        P("dp"),
        P("dp"),
        P("tensor", "dp"),
        P("dp"),
        P("dp", "tensor"),
        P("dp", "tensor"),
        P("tensor", "dp"),
    )
    return jax.shard_map(
        body,
        mesh=mesh,
        in_specs=placed,
        out_specs=(
            P(("dp", "tensor"), None),
            P("dp", None),
            P("dp"),
            P("dp", "tensor"),
            P("dp", "tensor"),
            P("dp", "tensor"),
            P("dp"),
            P("dp"),
            P("tensor", "dp"),
            P("dp"),
            P("dp", "tensor"),
            P("dp", "tensor"),
            P("tensor", "dp"),
        ),
        check_vma=False,
    )
```

```python
import functools

import jax
import jax.numpy as jnp
from jax import lax
from jax.experimental import pallas as pl
from jax.experimental.pallas import tpu as pltpu
from jax.sharding import PartitionSpec as P

HD = 64
LEN = 1024


EPSILON = 1e-05
ROPE_BASE = 1000000.0
MASKED = -1e30


def norm_rows(values, gain):
    return values * lax.rsqrt(jnp.mean(values * values, axis=-1, keepdims=True) + EPSILON) * gain


def rotate_half(values, cosine, sine_table):
    halfway = values.shape[-1] // 2
    first_half = values[..., :halfway]
    second_half = values[..., halfway:]
    return jnp.concatenate(
        [
            first_half * cosine - second_half * sine_table,
            second_half * cosine + first_half * sine_table,
        ],
        axis=-1,
    )


def rope_tables(positions):
    halfway = HD // 2
    frequency = ROPE_BASE ** (-(jnp.arange(halfway, dtype=jnp.float32) * 2.0 / HD))
    angle_grid = positions.astype(jnp.float32)[:, None] * frequency[None, :]
    return (jnp.cos(angle_grid)[:, None, :], jnp.sin(angle_grid)[:, None, :])


def matmul(left, right):
    return jnp.dot(left, right, preferred_element_type=jnp.float32)


def matmul_tn(left, right):
    return lax.dot_general(
        left, right, (((0,), (0,)), ((), ())), preferred_element_type=jnp.float32
    )


def matmul_nt(left, right):
    return lax.dot_general(
        left, right, (((1,), (1,)), ((), ())), preferred_element_type=jnp.float32
    )


def block_scores(query_block, key_rows, seq_segments, first_row, last_row):
    score_scale = query_block.shape[-1] ** (-0.5)
    places = jnp.arange(seq_segments.shape[0])
    scores = (
        jnp.einsum("tkgd,skd->kgts", query_block, key_rows, preferred_element_type=jnp.float32)
        * score_scale
    )
    allowed = (places[first_row:last_row, None] >= places[None, :last_row]) & (
        seq_segments[first_row:last_row, None] == seq_segments[None, :last_row]
    )
    return jnp.where(allowed, scores, MASKED)


def attend(operands):
    queries, keys_low, values_low, seq_segments = operands
    length = queries.shape[0]
    block_rows = min(512, length)
    pieces = []
    lse_parts = []
    for first_row in range(0, length, block_rows):
        last_row = first_row + block_rows
        scores = block_scores(
            queries[first_row:last_row], keys_low[:last_row], seq_segments, first_row, last_row
        )
        row_max = jnp.max(scores, axis=-1, keepdims=True)
        shifted = jnp.exp(scores - row_max)
        totals = jnp.sum(shifted, axis=-1, keepdims=True)
        probabilities = (shifted / totals).astype(jnp.bfloat16)
        pieces.append(
            jnp.einsum(
                "kgts,skd->tkgd",
                probabilities,
                values_low[:last_row],
                preferred_element_type=jnp.float32,
            )
        )
        lse_parts.append(row_max + jnp.log(totals))
    return (jnp.concatenate(pieces, axis=0), jnp.concatenate(lse_parts, axis=2))


def attend_back(operands, between):
    queries, keys_low, values_low, seq_segments, lse_rows, grad_mixed = operands
    length = queries.shape[0]
    block_rows = min(512, length)
    score_scale = queries.shape[-1] ** (-0.5)
    key_total = jnp.zeros(keys_low.shape, jnp.float32)
    value_total = jnp.zeros(values_low.shape, jnp.float32)
    query_pieces = []
    for first_row in reversed(range(0, length, block_rows)):
        if first_row == 0:
            key_total, value_total, grad_mixed, *between = lax.optimization_barrier(
                (key_total, value_total, grad_mixed, *between)
            )
        last_row = first_row + block_rows
        scores = block_scores(
            queries[first_row:last_row], keys_low[:last_row], seq_segments, first_row, last_row
        )
        probabilities = jnp.exp(scores - lse_rows[:, :, first_row:last_row])
        grad_block = grad_mixed[first_row:last_row]
        grad_probs = jnp.einsum(
            "tkgd,skd->kgts", grad_block, values_low[:last_row], preferred_element_type=jnp.float32
        )
        row_terms = jnp.sum(probabilities * grad_probs, axis=-1, keepdims=True)
        grad_scores = (probabilities * (grad_probs - row_terms)).astype(jnp.bfloat16)
        query_pieces.append(
            jnp.einsum(
                "kgts,skd->tkgd",
                grad_scores,
                keys_low[:last_row],
                preferred_element_type=jnp.float32,
            )
            * score_scale
        )
        padding = ((0, length - last_row), (0, 0), (0, 0))
        key_part = (
            jnp.einsum(
                "kgts,tkgd->skd",
                grad_scores,
                queries[first_row:last_row],
                preferred_element_type=jnp.float32,
            )
            * score_scale
        )
        value_part = jnp.einsum(
            "kgts,tkgd->skd",
            probabilities.astype(jnp.bfloat16),
            grad_block,
            preferred_element_type=jnp.float32,
        )
        key_total = key_total + jnp.pad(key_part, padding)
        value_total = value_total + jnp.pad(value_part, padding)
    return (jnp.concatenate(query_pieces[::-1], axis=0), key_total, value_total, between)


MESH = pl.DeviceIdType.MESH
VMEM_BYTES = 44 * 1024 * 1024


def block_of(ref, place, size):
    return ref.at[pl.ds(pl.multiple_of(place * size, size), size), :]


def greet(peers):
    barrier = pltpu.get_barrier_semaphore()
    for peer in peers:
        pl.semaphore_signal(barrier, inc=1, device_id=peer, device_id_type=MESH)
    pl.semaphore_wait(barrier, len(peers))


def dp_places(size):
    me = lax.axis_index("dp")
    return me // 2, lax.rem(me, 2), size // 2


def gather_kernel(size, count, *refs):
    shards, wholes = refs[:count], refs[count : 2 * count]
    own_sem, far_send, far_recv, near_send, near_recv = refs[2 * count :]
    column, side, columns = dp_places(size)
    near = {"dp": column * 2 + 1 - side}
    far = [{"dp": lax.rem(column + k, columns) * 2 + side} for k in range(1, columns)]
    greet([near] + far)
    mine = column * 2 + side
    started = []

    def slot(a, place):
        return block_of(wholes[a], place, shards[a].shape[0])

    for a in range(count):
        own = pltpu.make_async_copy(shards[a], slot(a, mine), own_sem.at[a])
        own.start()
        started.append(own.wait)
        copy = pltpu.make_async_remote_copy(
            src_ref=shards[a], dst_ref=slot(a, mine),
            send_sem=near_send.at[a, 0], recv_sem=near_recv.at[a, 0],
            device_id=near, device_id_type=MESH,
        )
        copy.start()
        started.append(copy.wait)
    arrivals = []
    for k in range(1, columns):
        for a in range(count):
            copy = pltpu.make_async_remote_copy(
                src_ref=shards[a], dst_ref=slot(a, mine),
                send_sem=far_send.at[a, k - 1], recv_sem=far_recv.at[a, k - 1],
                device_id=far[k - 1], device_id_type=MESH,
            )
            copy.start()
            started.append(copy.wait_send)
            arrivals.append((k, a))
    for k, a in arrivals:
        place = lax.rem(column + columns - k, columns) * 2 + side
        landed = pltpu.make_async_remote_copy(
            src_ref=shards[a], dst_ref=slot(a, place),
            send_sem=far_send.at[a, k - 1], recv_sem=far_recv.at[a, k - 1],
            device_id=near, device_id_type=MESH,
        )
        landed.wait_recv()
        copy = pltpu.make_async_remote_copy(
            src_ref=slot(a, place), dst_ref=slot(a, place),
            send_sem=near_send.at[a, k], recv_sem=near_recv.at[a, k],
            device_id=near, device_id_type=MESH,
        )
        copy.start()
        started.append(copy.wait)
    for wait in started:
        wait()


def gather_dp(arrays, collective_id):
    size = lax.axis_size("dp")
    columns, count = size // 2, len(arrays)
    shapes = [
        jax.ShapeDtypeStruct((size * array.shape[0], array.shape[1]), array.dtype)
        for array in arrays
    ]
    dma = pltpu.SemaphoreType.DMA
    return pl.pallas_call(
        functools.partial(gather_kernel, size, count),
        out_shape=tuple(shapes),
        in_specs=[pl.BlockSpec(memory_space=pl.ANY)] * count,
        out_specs=tuple([pl.BlockSpec(memory_space=pl.ANY)] * count),
        scratch_shapes=[
            dma((count,)),
            dma((count, columns - 1)),
            dma((count, columns - 1)),
            dma((count, columns)),
            dma((count, columns)),
        ],
        compiler_params=pltpu.CompilerParams(collective_id=collective_id, has_side_effects=True),
        cost_estimate=pl.CostEstimate(flops=0, bytes_accessed=80_000_000, transcendentals=0),
    )(*arrays)


def scatter_kernel(size, count, later, *refs):
    parts, refs = refs[:count], refs[later:]
    sums = refs[count : 2 * count]
    near_slots = refs[2 * count : 3 * count]
    leaving = refs[3 * count : 4 * count]
    far_slots = refs[4 * count : 5 * count]
    near_send, near_recv, far_send, far_recv = refs[5 * count :]
    column, side, columns = dp_places(size)
    near = {"dp": column * 2 + 1 - side}
    far = [{"dp": lax.rem(column + k, columns) * 2 + side} for k in range(1, columns)]
    greet([near] + far)
    order = [(k, a) for k in list(range(1, columns)) + [0] for a in range(count)]

    def part(a, place):
        return block_of(parts[a], place, sums[a].shape[0])

    near_copies, far_copies = {}, {}
    for k, a in order:
        place = lax.rem(column + k, columns) * 2 + 1 - side
        copy = pltpu.make_async_remote_copy(
            src_ref=part(a, place), dst_ref=near_slots[a].at[k],
            send_sem=near_send.at[a, k], recv_sem=near_recv.at[a, k],
            device_id=near, device_id_type=MESH,
        )
        copy.start()
        near_copies[k, a] = copy
    for k, a in order:
        near_copies[k, a].wait_recv()
        place = lax.rem(column + k, columns) * 2 + side
        total = part(a, place)[...].astype(jnp.float32) + near_slots[a][k].astype(jnp.float32)
        if k == 0:
            sums[a][...] = total
            continue
        leaving[a][k - 1] = total.astype(jnp.bfloat16)
        copy = pltpu.make_async_remote_copy(
            src_ref=leaving[a].at[k - 1], dst_ref=far_slots[a].at[k - 1],
            send_sem=far_send.at[a, k - 1], recv_sem=far_recv.at[a, k - 1],
            device_id=far[k - 1], device_id_type=MESH,
        )
        copy.start()
        far_copies[k, a] = copy
    for k, a in order:
        if k > 0:
            far_copies[k, a].wait_recv()
            sums[a][...] += far_slots[a][k - 1].astype(jnp.float32)
    for k, a in order:
        near_copies[k, a].wait_send()
        if k > 0:
            far_copies[k, a].wait_send()


def scatter_dp(arrays, after, collective_id):
    size = lax.axis_size("dp")
    columns, count = size // 2, len(arrays)
    shapes = [(array.shape[0] // size, array.shape[1]) for array in arrays]
    dma = pltpu.SemaphoreType.DMA
    return pl.pallas_call(
        functools.partial(scatter_kernel, size, count, len(after)),
        out_shape=tuple(jax.ShapeDtypeStruct(shape, jnp.float32) for shape in shapes),
        in_specs=[pl.BlockSpec(memory_space=pltpu.VMEM)] * count
        + [pl.BlockSpec(memory_space=pl.ANY)] * len(after),
        out_specs=tuple([pl.BlockSpec(memory_space=pltpu.VMEM)] * count),
        scratch_shapes=[pltpu.VMEM((columns,) + shape, jnp.bfloat16) for shape in shapes]
        + [pltpu.VMEM((columns - 1,) + shape, jnp.bfloat16) for shape in shapes]
        + [pltpu.VMEM((columns - 1,) + shape, jnp.bfloat16) for shape in shapes]
        + [
            dma((count, columns)),
            dma((count, columns)),
            dma((count, columns - 1)),
            dma((count, columns - 1)),
        ],
        compiler_params=pltpu.CompilerParams(
            collective_id=collective_id, has_side_effects=True, vmem_limit_bytes=VMEM_BYTES
        ),
        cost_estimate=pl.CostEstimate(flops=0, bytes_accessed=80_000_000, transcendentals=0),
    )(*arrays, *after)


def total_kernel(size, dp_size, later, swaps, *refs):
    part, small, whole, small_sum = refs[0], refs[1], refs[2 + later], refs[3 + later]
    parts, swapped = refs[2 : 2 + later], refs[4 + later]
    swap_send, swap_recv = refs[-2:]
    (near_slots, leaving, far_slots, small_slots, near_send, near_recv, far_send, far_recv,
     back_send, back_recv, on_send, on_recv, small_send, small_recv) = refs[5 + later : -2]
    me = lax.axis_index("tensor")
    column, side, columns = me // 2, lax.rem(me, 2), size // 2
    share = whole.shape[0] // size
    near = {"tensor": column * 2 + 1 - side}
    far = [{"tensor": lax.rem(column + k, columns) * 2 + side} for k in range(1, columns)]
    others = [{"tensor": lax.rem(me + k, size)} for k in range(1, size)]
    dp_column, dp_side, dp_columns = dp_places(dp_size)
    twin = {"dp": dp_column * 2 + 1 - dp_side}
    greet(others + [twin] if swaps else others)

    def rows(ref, place):
        return block_of(ref, place, share)

    small_copies = []
    for k in range(1, size):
        copy = pltpu.make_async_remote_copy(
            src_ref=small, dst_ref=small_slots.at[k - 1],
            send_sem=small_send.at[k - 1], recv_sem=small_recv.at[k - 1],
            device_id=others[k - 1], device_id_type=MESH,
        )
        small_copies.append(copy)
    near_copies, far_copies, started = [], [], []
    order = list(range(1, columns)) + [0]
    for k in order:
        place = lax.rem(column + k, columns) * 2 + 1 - side
        copy = pltpu.make_async_remote_copy(
            src_ref=rows(part, place), dst_ref=near_slots.at[k],
            send_sem=near_send.at[k], recv_sem=near_recv.at[k],
            device_id=near, device_id_type=MESH,
        )
        copy.start()
        near_copies.append(copy)
    for copy in small_copies:
        copy.start()
    for index, step in enumerate(swaps):
        place = lax.rem(dp_column + step, dp_columns) * 2 + 1 - dp_side
        for a in range(later):
            rows_each = parts[a].shape[0] // dp_size
            copy = pltpu.make_async_remote_copy(
                src_ref=block_of(parts[a], place, rows_each),
                dst_ref=swapped.at[index, pl.ds(a * rows_each, rows_each), :],
                send_sem=swap_send.at[index, a], recv_sem=swap_recv.at[index, a],
                device_id=twin, device_id_type=MESH,
            )
            copy.start()
            started.append(copy.wait)
    mine = rows(whole, me)
    for k, arrived in zip(order, near_copies):
        arrived.wait_recv()
        place = lax.rem(column + k, columns) * 2 + side
        total = rows(part, place)[...].astype(jnp.float32) + near_slots[k].astype(jnp.float32)
        if k > 0:
            leaving[k - 1] = total.astype(jnp.bfloat16)
            copy = pltpu.make_async_remote_copy(
                src_ref=leaving.at[k - 1], dst_ref=far_slots.at[k - 1],
                send_sem=far_send.at[k - 1], recv_sem=far_recv.at[k - 1],
                device_id=far[k - 1], device_id_type=MESH,
            )
            copy.start()
            far_copies.append(copy)
    for copy in far_copies:
        copy.wait_recv()
    for k in range(1, columns):
        total = total + far_slots[k - 1].astype(jnp.float32)
    mine[...] = total.astype(jnp.bfloat16)
    for k in range(1, columns):
        copy = pltpu.make_async_remote_copy(
            src_ref=mine, dst_ref=rows(whole, me),
            send_sem=back_send.at[k - 1], recv_sem=back_recv.at[k - 1],
            device_id=far[k - 1], device_id_type=MESH,
        )
        copy.start()
        started.append(copy.wait_send)
    copy = pltpu.make_async_remote_copy(
        src_ref=mine, dst_ref=rows(whole, me),
        send_sem=on_send.at[0], recv_sem=on_recv.at[0],
        device_id=near, device_id_type=MESH,
    )
    copy.start()
    started.append(copy.wait)
    for copy in small_copies:
        copy.wait_recv()
    small_total = small[...]
    for k in range(1, size):
        small_total = small_total + small_slots[k - 1]
    small_sum[...] = small_total
    for k in range(1, columns):
        place = lax.rem(column + columns - k, columns) * 2 + side
        landed = pltpu.make_async_remote_copy(
            src_ref=mine, dst_ref=rows(whole, place),
            send_sem=back_send.at[k - 1], recv_sem=back_recv.at[k - 1],
            device_id=near, device_id_type=MESH,
        )
        landed.wait_recv()
        copy = pltpu.make_async_remote_copy(
            src_ref=rows(whole, place), dst_ref=rows(whole, place),
            send_sem=on_send.at[k], recv_sem=on_recv.at[k],
            device_id=near, device_id_type=MESH,
        )
        copy.start()
        started.append(copy.wait)
    for wait in started:
        wait()
    for copy in near_copies + far_copies + small_copies:
        copy.wait_send()


def total_tensor(part, small, after, swaps, collective_id):
    size = lax.axis_size("tensor")
    columns = size // 2
    length, width = part.shape
    share = length // size
    dp_size = lax.axis_size("dp")
    if swaps:
        rows = len(after) * after[0].shape[0] // dp_size
        swapped = jax.ShapeDtypeStruct((len(swaps), rows, after[0].shape[1]), jnp.bfloat16)
    else:
        swapped = jax.ShapeDtypeStruct((1, 16, 128), jnp.bfloat16)
    dma = pltpu.SemaphoreType.DMA
    return pl.pallas_call(
        functools.partial(total_kernel, size, dp_size, len(after), swaps),
        out_shape=(
            jax.ShapeDtypeStruct(part.shape, jnp.bfloat16),
            jax.ShapeDtypeStruct(small.shape, jnp.float32),
            swapped,
        ),
        in_specs=[pl.BlockSpec(memory_space=pltpu.VMEM)] * 2
        + [pl.BlockSpec(memory_space=pl.ANY)] * len(after),
        out_specs=tuple([pl.BlockSpec(memory_space=pltpu.VMEM)] * 2)
        + (pl.BlockSpec(memory_space=pl.ANY),),
        scratch_shapes=[
            pltpu.VMEM((columns, share, width), jnp.bfloat16),
            pltpu.VMEM((columns - 1, share, width), jnp.bfloat16),
            pltpu.VMEM((columns - 1, share, width), jnp.bfloat16),
            pltpu.VMEM((size - 1,) + small.shape, jnp.float32),
            dma((columns,)),
            dma((columns,)),
            dma((columns - 1,)),
            dma((columns - 1,)),
            dma((columns - 1,)),
            dma((columns - 1,)),
            dma((columns,)),
            dma((columns,)),
            dma((size - 1,)),
            dma((size - 1,)),
            dma((max(len(swaps), 1), max(len(after), 1))),
            dma((max(len(swaps), 1), max(len(after), 1))),
        ],
        compiler_params=pltpu.CompilerParams(
            collective_id=collective_id, has_side_effects=True, vmem_limit_bytes=VMEM_BYTES
        ),
        cost_estimate=pl.CostEstimate(flops=0, bytes_accessed=80_000_000, transcendentals=0),
    )(part, small, *after)


def shifted_pairs(size, step):
    return [(place, (place + 2 * step) % size) for place in range(size)]


def swapped_pairs(size):
    return [(place, place ^ 1) for place in range(size)]


def gather_start(shard):
    size = lax.axis_size("dp")
    columns = size // 2
    middle = columns // 2
    blocks = {0: shard}
    for step in range(1, columns):
        if step != middle:
            blocks[step] = lax.ppermute(shard, "dp", shifted_pairs(size, step))
    first = [step for step in blocks if step > 0]
    held, *came = lax.optimization_barrier((shard, *[blocks[step] for step in first]))
    blocks.update(zip(first, came))
    blocks[middle] = lax.ppermute(held, "dp", shifted_pairs(size, middle))
    return [blocks[step] for step in range(columns)], came


def gather_end(blocks, twins, count):
    size = lax.axis_size("dp")
    column, side, columns = dp_places(size)
    rows = blocks[0].shape[0] // count
    wholes = []
    for a in range(count):
        whole = jnp.zeros((size * rows, blocks[0].shape[1]), blocks[0].dtype)
        for step in range(columns):
            base = lax.rem(column + columns - step, columns) * 2
            for held, place in ((blocks[step], base + side), (twins[step], base + 1 - side)):
                whole = lax.dynamic_update_slice_in_dim(
                    whole, held[a * rows : (a + 1) * rows], place * rows, 0
                )
        wholes.append(whole)
    return wholes


def swap_sides(block):
    return lax.ppermute(block, "dp", swapped_pairs(lax.axis_size("dp")))


def blocks_for(parts, place, rows):
    return jnp.concatenate(
        [lax.dynamic_slice_in_dim(part, place * rows, rows, 0) for part in parts], axis=0
    )


def scatter_start(parts, swapped):
    size = lax.axis_size("dp")
    column, side, columns = dp_places(size)
    rows = parts[0].shape[0] // size

    sums = []
    for step in range(1, columns):
        base = lax.rem(column + step, columns) * 2
        if step <= swapped.shape[0]:
            came = swapped[step - 1]
        else:
            came = swap_sides(blocks_for(parts, base + 1 - side, rows))
        both = blocks_for(parts, base + side, rows).astype(jnp.float32) + came.astype(jnp.float32)
        sums.append(both.astype(jnp.bfloat16))
    return sums


def scatter_step(block, step):
    return lax.ppermute(block, "dp", shifted_pairs(lax.axis_size("dp"), step))


def pack_rows(rows):
    padded = [jnp.pad(row, (0, 128 - row.shape[0])) for row in rows]
    padded = padded + [jnp.zeros_like(padded[0])] * (16 - len(padded))
    return jnp.stack(padded)


def pack_sums(vectors, size):
    blocks = []
    for vector in vectors:
        share = vector.reshape(size, -1)
        blocks.append(jnp.pad(share, ((0, 0), (0, 128 - share.shape[1]))))
    blocks = blocks + [jnp.zeros_like(blocks[0])] * (16 - len(blocks))
    return jnp.stack(blocks, axis=1).reshape(size * 16, 128).astype(jnp.bfloat16)


def swiglu(gate_in, up_in):
    return jax.nn.silu(gate_in) * up_in


def body(
    tokens,
    cotangent,
    segments,
    positions,
    attn_gain,
    w_query,
    w_key,
    w_value,
    query_gain,
    key_gain,
    w_out,
    ffn_gain,
    w_gate,
    w_up,
    w_down,
):
    dp_size = lax.axis_size("dp")
    gain_tile = pack_rows([attn_gain, ffn_gain, query_gain, key_gain])
    gain_tiles, query_full, key_full, value_full, out_full = gather_dp(
        (gain_tile, w_query, w_key, w_value, w_out.T), 1
    )
    gain_tiles, *ffn_shards = lax.optimization_barrier((gain_tiles, w_gate, w_up, w_down.T))
    ffn_shard = jnp.concatenate(ffn_shards, axis=0)
    columns = dp_size // 2
    ffn_blocks, ffn_first = gather_start(ffn_shard)
    ffn_twins = [swap_sides(ffn_shard)]
    gain_tiles = gain_tiles.reshape(dp_size, 16, 128)
    gain_first = gain_tiles[:, 0, : attn_gain.shape[0]].reshape(-1)
    gain_second = gain_tiles[:, 1, : ffn_gain.shape[0]].reshape(-1)
    qgain_full = gain_tiles[:, 2, : query_gain.shape[0]].reshape(-1)
    kgain_full = gain_tiles[:, 3, : key_gain.shape[0]].reshape(-1)
    no_small = jnp.zeros((8, 128), jnp.float32)
    token_count = tokens.shape[0]
    seq_count = token_count // LEN
    local_heads = query_full.shape[1] // HD
    local_kv = key_full.shape[1] // HD
    group_size = local_heads // local_kv
    share_rows = token_count // lax.axis_size("tensor")
    own_start = lax.axis_index("tensor") * share_rows
    inputs = tokens.astype(jnp.float32)
    attn_scale = gain_first.astype(jnp.float32)
    normed_float, attn_norm_back = jax.vjp(norm_rows, inputs, attn_scale)
    normed = normed_float.astype(jnp.bfloat16)
    query_raw = matmul(normed, query_full).reshape(token_count, local_heads, HD)
    key_raw = matmul(normed, key_full).reshape(token_count, local_kv, HD)
    value_low = (
        matmul(normed, value_full).astype(jnp.bfloat16).reshape(seq_count, LEN, local_kv, HD)
    )
    cosine, sine_table = rope_tables(positions)

    def head_prep(raw_rows, gain_rows):
        return rotate_half(norm_rows(raw_rows, gain_rows), cosine, sine_table)

    query_prep, query_back = jax.vjp(head_prep, query_raw, qgain_full.astype(jnp.float32))
    key_prep, key_back = jax.vjp(head_prep, key_raw, kgain_full.astype(jnp.float32))
    query_low = query_prep.astype(jnp.bfloat16).reshape(seq_count, LEN, local_kv, group_size, HD)
    key_low = key_prep.astype(jnp.bfloat16).reshape(seq_count, LEN, local_kv, HD)
    seq_segments = segments.reshape(seq_count, LEN)
    mixed, lse_rows = lax.map(attend, (query_low, key_low, value_low, seq_segments))
    mixed_low = mixed.reshape(token_count, local_heads * HD).astype(jnp.bfloat16)
    attn_part = matmul_nt(mixed_low, out_full).astype(jnp.bfloat16)
    ffn_scale = gain_second.astype(jnp.float32)
    attn_total, _, _ = total_tensor(attn_part, no_small, ffn_first, (), 3)
    ffn_twins += [swap_sides(block) for block in ffn_blocks[1:]]
    gate_full, up_full, down_full = gather_end(ffn_blocks, ffn_twins, 3)
    residual = inputs + attn_total.astype(jnp.float32)
    ffn_float, ffn_norm_back = jax.vjp(norm_rows, residual, ffn_scale)
    normed_ffn = ffn_float.astype(jnp.bfloat16)
    residual_rows = lax.dynamic_slice_in_dim(residual, own_start, share_rows, 0)
    gate_value = matmul(normed_ffn, gate_full)
    up_value = matmul(normed_ffn, up_full)
    hidden_float, swiglu_back = jax.vjp(swiglu, gate_value, up_value)
    hidden = hidden_float.astype(jnp.bfloat16)
    ffn_share = lax.psum_scatter(
        matmul_nt(
            lax.slice_in_dim(hidden, 0, share_rows * lax.axis_size("tensor"), axis=0), down_full
        ).astype(jnp.bfloat16),
        "tensor",
        scatter_dimension=0,
        tiled=True,
    ).astype(jnp.float32)
    output = (residual_rows + ffn_share).astype(jnp.bfloat16)
    grad_output = cotangent.astype(jnp.float32)
    down_grad = matmul_tn(cotangent, hidden)
    grad_hidden = matmul(cotangent, down_full)
    grad_gate, grad_up = swiglu_back(grad_hidden)
    gate_low = grad_gate.astype(jnp.bfloat16)
    up_low = grad_up.astype(jnp.bfloat16)
    gate_grad = matmul_tn(normed_ffn, gate_low)
    up_grad = matmul_tn(normed_ffn, up_low)
    ffn_input_part = matmul_nt(gate_low, gate_full) + matmul_nt(up_low, up_full)
    ffn_parts = [grad.astype(jnp.bfloat16) for grad in (gate_grad, up_grad, down_grad)]
    early = min(2, columns - 1)
    ffn_input_grad, _, ffn_swapped = total_tensor(
        ffn_input_part.astype(jnp.bfloat16), no_small, ffn_parts, tuple(range(1, early + 1)), 4
    )
    ffn_sums = scatter_start(ffn_parts, ffn_swapped)
    residual_part, ffn_gain_part = ffn_norm_back(ffn_input_grad.astype(jnp.float32))
    grad_residual = residual_part + grad_output
    grad_attn_low = grad_residual.astype(jnp.bfloat16)
    out_grad = matmul_tn(grad_attn_low, mixed_low)
    grad_mixed = (
        matmul(grad_attn_low, out_full)
        .astype(jnp.bfloat16)
        .reshape(seq_count, LEN, local_kv, group_size, HD)
    )
    ffn_came = {step: scatter_step(ffn_sums[step - 1], step) for step in range(1, early + 1)}
    between = [ffn_came[1]] + ffn_sums[early : columns - 1]
    pieces = []
    for seq in range(seq_count):
        *piece, between = attend_back(
            [
                array[seq]
                for array in (query_low, key_low, value_low, seq_segments, lse_rows, grad_mixed)
            ],
            between,
        )
        pieces.append(piece)
    grad_query, grad_key, grad_value = (jnp.stack(piece) for piece in zip(*pieces))
    ffn_came[1] = between[0]
    for step in range(early + 1, columns):
        ffn_came[step] = scatter_step(between[step - early], step)
    ffn_came = [ffn_came[step] for step in range(1, columns)]
    grad_qraw, grad_qgain = query_back(grad_query.reshape(token_count, local_heads, HD))
    grad_kraw, grad_kgain = key_back(grad_key.reshape(token_count, local_kv, HD))
    query_low_grad = grad_qraw.reshape(token_count, local_heads * HD).astype(jnp.bfloat16)
    key_low_grad = grad_kraw.reshape(token_count, local_kv * HD).astype(jnp.bfloat16)
    value_low_grad = grad_value.reshape(token_count, local_kv * HD).astype(jnp.bfloat16)
    query_weight_grad = matmul_tn(normed, query_low_grad)
    key_weight_grad = matmul_tn(normed, key_low_grad)
    value_weight_grad = matmul_tn(normed, value_low_grad)
    attn_input_part = (
        matmul_nt(query_low_grad, query_full)
        + matmul_nt(key_low_grad, key_full)
        + matmul_nt(value_low_grad, value_full)
    )
    gain_sums = jnp.pad(
        jnp.stack([grad_qgain, grad_kgain]), ((0, 6), (0, 128 - grad_qgain.shape[0]))
    )
    attn_input_grad, gain_sums, ffn_swapped = total_tensor(
        attn_input_part.astype(jnp.bfloat16), gain_sums, ffn_parts, (0,), 5
    )
    qgain_total = gain_sums[0, : grad_qgain.shape[0]]
    kgain_total = gain_sums[1, : grad_kgain.shape[0]]
    input_part, attn_gain_grad = attn_norm_back(attn_input_grad.astype(jnp.float32))
    tokens_grad = input_part + grad_residual
    ffn_own = blocks_for(ffn_parts, lax.axis_index("dp"), ffn_parts[0].shape[0] // dp_size)
    ffn_total = ffn_own.astype(jnp.float32) + ffn_swapped[0].astype(jnp.float32)
    for block in ffn_came:
        ffn_total = ffn_total + block.astype(jnp.float32)
    ffn_grads = jnp.split(ffn_total, 3)
    gain_grads = pack_sums([attn_gain_grad, ffn_gain_part, qgain_total, kgain_total], dp_size)
    attn_grads = scatter_dp(
        [gain_grads]
        + [
            grad.astype(jnp.bfloat16)
            for grad in (query_weight_grad, key_weight_grad, value_weight_grad, out_grad)
        ],
        ffn_came[1:],
        7,
    )
    gain_grads = attn_grads[0]
    return (
        output,
        tokens_grad,
        gain_grads[0, : attn_gain.shape[0]],
        attn_grads[1],
        attn_grads[2],
        attn_grads[3],
        gain_grads[2, : query_gain.shape[0]],
        gain_grads[3, : key_gain.shape[0]],
        attn_grads[4].T,
        gain_grads[1, : ffn_gain.shape[0]],
        ffn_grads[0],
        ffn_grads[1],
        ffn_grads[2].T,
    )


def solution(mesh):
    placed = (
        P("dp", None),
        P("dp", None),
        P("dp"),
        P("dp"),
        P("dp"),
        P("dp", "tensor"),
        P("dp", "tensor"),
        P("dp", "tensor"),
        P("dp"),
        P("dp"),
        P("tensor", "dp"),
        P("dp"),
        P("dp", "tensor"),
        P("dp", "tensor"),
        P("tensor", "dp"),
    )
    return jax.shard_map(
        body,
        mesh=mesh,
        in_specs=placed,
        out_specs=(
            P(("dp", "tensor"), None),
            P("dp", None),
            P("dp"),
            P("dp", "tensor"),
            P("dp", "tensor"),
            P("dp", "tensor"),
            P("dp"),
            P("dp"),
            P("tensor", "dp"),
            P("dp"),
            P("dp", "tensor"),
            P("dp", "tensor"),
            P("tensor", "dp"),
        ),
        check_vma=False,
    )
```
